32 devices in a mesh: dp: 4 (over y, x), pipe: 2 (over core), tensor: 4 (over z).
Axes of the slice: x: 2, y: 2, z: 4, core: 2. Of those that a mesh axis runs over, the one named last changes fastest.
Arguments:
- inputs: bfloat16 [2, 896, 8192], P('pipe', 'dp', 'tensor'), may hold values from -6 to 6
- cotangent: bfloat16 [896, 8192], P('dp', 'tensor'), may hold values from -6 to 6
- up_first: bfloat16 [2, 32, 256, 256], P('pipe', 'tensor'), may hold values from -0.375 to 0.375
- up_second: bfloat16 [2, 32, 256, 1024], P('pipe', 'tensor'), may hold values from -0.375 to 0.375
- down_first: bfloat16 [2, 32, 1024, 256], P('pipe', 'tensor'), may hold values from -0.1875 to 0.1875
- down_second: bfloat16 [2, 32, 256, 256], P('pipe', 'tensor'), may hold values from -0.375 to 0.375
Outputs:
- grad_inputs: bfloat16 [2, 896, 8192], P('pipe', 'dp', 'tensor')
- grad_up_first: float32 [2, 32, 256, 256], P('pipe', 'tensor', 'dp')
- grad_up_second: float32 [2, 32, 256, 1024], P('pipe', 'tensor', 'dp')
- grad_down_first: float32 [2, 32, 1024, 256], P('pipe', 'tensor', 'dp')
- grad_down_second: float32 [2, 32, 256, 256], P('pipe', 'tensor', 'dp')
The draws below stay inside these ranges and needn't reach their ends.
All inputs are finite; a program needn't handle non-finite values.
Results may differ from the reference program's by a relative error of at most 0.018.
Values may be sent and summed in bfloat16 or wider, within the bound.
A program may use at most 128 MiB of HBM per device.

```python
import math
import jax
import jax.numpy as jnp

NB = 32
BS = 256
HB = 1024
D = 8192
LAYERS = 2
TOKENS = 896


def level_of(key, dims, shards, smallest, largest):
    gain = 1.0
    for axis_at, parts in shards:
        steps = jax.random.uniform(jax.random.fold_in(jax.random.fold_in(key, 6), axis_at), (parts,), jnp.float32, smallest / len(shards), largest / len(shards))
        gain = gain * jnp.repeat(jnp.exp(steps), dims[axis_at] // parts).reshape((-1,) + (1,) * (len(dims) - 1 - axis_at))
    return gain


def noise(own_key, dims, deviation, limit, cuts=(), kind=jnp.bfloat16):
    values = jax.random.normal(own_key, dims, jnp.float32) * deviation
    if len(cuts) > 0:
        values = level_of(own_key, dims, cuts, -0.22, 0.18) * values
    return jnp.clip(values, min=-limit, max=limit).astype(kind)


def setup_inputs(seed: int = 0) -> dict:
    splits = jax.random.split(jax.random.key(seed), 7)
    return {
        "inputs": noise(splits[0], (LAYERS, TOKENS, D), 1.0, 6.0, ((0, 2), (1, 4), (2, 4))),
        "cotangent": noise(splits[1], (TOKENS, D), 1.0, 6.0, ((0, 4), (1, 4))),
        "up_first": noise(splits[2], (LAYERS, NB, BS, BS), BS ** -0.5, 0.375, ((0, 2), (1, 4))),
        "up_second": noise(splits[3], (LAYERS, NB, BS, HB), BS ** -0.5, 0.375, ((0, 2), (1, 4))),
        "down_first": noise(splits[4], (LAYERS, NB, HB, BS), HB ** -0.5, 0.1875, ((0, 2), (1, 4))),
        "down_second": noise(splits[5], (LAYERS, NB, BS, BS), BS ** -0.5, 0.375, ((0, 2), (1, 4))),
    }


root_half = 1.0 / math.sqrt(2.0)
norm_density = 1.0 / math.sqrt(2.0 * math.pi)

def gelu_value(values):
    return values * 0.5 * (1.0 + jax.scipy.special.erf(values * root_half))

def gelu_slope(values):
    cumulative = 0.5 * (1.0 + jax.scipy.special.erf(values * root_half))
    return cumulative + values * jnp.exp(-0.5 * values * values) * norm_density

def permute(matrix):
    row_count = matrix.shape[0]
    shaped = matrix.reshape(row_count, NB, NB, BS // NB).transpose(0, 2, 1, 3)
    return shaped.reshape(row_count, NB * BS)

def block_apply(matrix, weight):
    row_count = matrix.shape[0]
    shaped = matrix.astype(jnp.float32).reshape(row_count, NB, -1)
    result = jnp.einsum('tic,ice->tie', shaped, weight.astype(jnp.float32))
    return result.reshape(row_count, -1)

def block_apply_back(matrix, weight):
    row_count = matrix.shape[0]
    shaped = matrix.astype(jnp.float32).reshape(row_count, NB, -1)
    result = jnp.einsum('tie,ice->tic', shaped, weight.astype(jnp.float32))
    return result.reshape(row_count, -1)

def weight_grad(left, right, factor):
    row_count = left.shape[0]
    left_blocks = left.astype(jnp.float32).reshape(row_count, NB, -1)
    right_blocks = right.astype(jnp.float32).reshape(row_count, NB, -1)
    return jnp.einsum('tic,tie->ice', left_blocks, right_blocks) * factor

def reference(inputs, cotangent, up_first, up_second, down_first, down_second):
    factor = 1.0 / math.sqrt(TOKENS)
    incoming = cotangent
    grads_x, grads_a, grads_b, grads_c, grads_d = ([], [], [], [], [])
    for layer in range(LAYERS - 1, -1, -1):
        acts = inputs[layer]
        first = block_apply(acts, up_first[layer]).astype(jnp.bfloat16)
        mixed = permute(first)
        pre = block_apply(mixed, up_second[layer])
        hidden = gelu_value(pre).astype(jnp.bfloat16)
        down = block_apply(hidden, down_first[layer]).astype(jnp.bfloat16)
        last = permute(down)
        grad_last = block_apply_back(incoming, down_second[layer]).astype(jnp.bfloat16)
        grad_down = permute(grad_last)
        grad_hidden = block_apply_back(grad_down, down_first[layer])
        grad_pre = (grad_hidden * gelu_slope(pre)).astype(jnp.bfloat16)
        grad_mixed = block_apply_back(grad_pre, up_second[layer]).astype(jnp.bfloat16)
        grad_first = permute(grad_mixed)
        grad_acts = (incoming.astype(jnp.float32) + block_apply_back(grad_first, up_first[layer])).astype(jnp.bfloat16)
        grads_x.append(grad_acts)
        grads_a.append(weight_grad(acts, grad_first, factor))
        grads_b.append(weight_grad(mixed, grad_pre, factor))
        grads_c.append(weight_grad(hidden, grad_down, factor))
        grads_d.append(weight_grad(last, incoming, factor))
        incoming = grad_acts
    return (jnp.stack(grads_x[::-1]), jnp.stack(grads_a[::-1]), jnp.stack(grads_b[::-1]), jnp.stack(grads_c[::-1]), jnp.stack(grads_d[::-1]))
```

```python
import math

import jax
import jax.numpy as jnp
from jax import lax
from jax.experimental import pallas as pl
from jax.experimental.pallas import tpu as pltpu
from jax.sharding import PartitionSpec as P

MESH = pl.DeviceIdType.MESH
root_half = 1.0 / math.sqrt(2.0)
norm_density = 1.0 / math.sqrt(2.0 * math.pi)
lanes = 128
f32 = jnp.float32
bf16 = jnp.bfloat16


def mm(left, right, left_dim, right_dim):
    return lax.dot_general(
        left, right, (((left_dim,), (right_dim,)), ((), ())), preferred_element_type=f32
    )


def make_kernel(sizes, factor):
    nt, nd, ns, lb, bs, hb, tp = sizes
    stride = bs // (nt * lb)
    rows = lb * stride

    def kernel(
        x_ref, cot_ref, w1, w2, w3, w4,
        gout, r1, r2, r3, r4,
        gbuf, sbuf, rbuf, hidden, slope, gpre, st1, st2, st3, st4,
        a_send, a_recv, d_send, d_recv, own_sem, p_send, p_recv,
    ):
        me_t = lax.axis_index("tensor")
        me_d = lax.axis_index("dp")
        me_s = lax.axis_index("pipe")
        is_last = me_s == ns - 1
        not_last = me_s < ns - 1
        not_first = me_s > 0

        barrier = pltpu.get_barrier_semaphore()
        for k in range(1, nt):
            pl.semaphore_signal(
                barrier, inc=1, device_id={"tensor": lax.rem(me_t + k, nt)}, device_id_type=MESH
            )
        for k in range(1, nd):
            pl.semaphore_signal(
                barrier, inc=1, device_id={"dp": lax.rem(me_d + k, nd)}, device_id_type=MESH
            )

        for k in range(1, ns):
            pl.semaphore_signal(
                barrier, inc=1, device_id={"pipe": lax.rem(me_s + k, ns)}, device_id_type=MESH
            )
        pl.semaphore_wait(barrier, nt - 1 + nd - 1 + ns - 1)

        def cols(i):
            return pl.ds(pl.multiple_of(i * bs, bs), bs)

        def produce(which, make):
            def pair(p, carry):
                parts = [make(2 * p + u).reshape(nt, lb, stride, tp) for u in range(2)]
                both = jnp.concatenate(parts, axis=2).astype(bf16)
                at = pl.multiple_of(p * 2 * stride, 2 * stride)
                sbuf[which, :, :, pl.ds(at, 2 * stride), :] = both
                return carry

            lax.fori_loop(0, lb // 2, pair, 0)

        def a2a(which, k):
            peer = lax.rem(me_t + k, nt)
            return pltpu.make_async_remote_copy(
                src_ref=sbuf.at[which, peer],
                dst_ref=rbuf.at[which, me_t],
                send_sem=a_send.at[which, k],
                recv_sem=a_recv.at[which, k],
                device_id={"tensor": peer},
                device_id_type=MESH,
            )

        def send(which):
            for k in range(1, nt):
                a2a(which, k).start()
            rbuf[which, me_t] = sbuf[which, me_t]

        def arrive(which):
            for k in range(1, nt):
                a2a(which, k).wait_recv()

        def block(which, j):
            return rbuf[which, :, j].reshape(bs, tp)

        pairs = ((st1, r1), (st2, r2), (st3, r3), (st4, r4))

        def share(which, k):
            staged, landed = pairs[which]
            peer = lax.rem(me_d + k, nd)
            return pltpu.make_async_remote_copy(
                src_ref=staged.at[peer],
                dst_ref=landed.at[me_d],
                send_sem=d_send.at[which, k],
                recv_sem=d_recv.at[which, k],
                device_id={"dp": peer},
                device_id_type=MESH,
            )

        def own(which):
            staged, landed = pairs[which]
            return pltpu.make_async_copy(staged.at[me_d], landed.at[me_d], own_sem.at[which])

        def spread(which):
            for k in range(1, nd):
                share(which, k).start()
            own(which).start()

        def hand_on():
            return pltpu.make_async_remote_copy(
                src_ref=gout,
                dst_ref=gbuf,
                send_sem=p_send,
                recv_sem=p_recv,
                device_id={"pipe": lax.rem(me_s + ns - 1, ns)},
                device_id_type=MESH,
            )

        def make_first(i):
            return mm(w1[i], x_ref[:, cols(i)], 0, 1)

        def make_grad_last(i):
            return mm(w4[i], gbuf[:, cols(i)], 1, 1)

        def make_down(j):
            return mm(w3[j], hidden[j], 0, 0)

        def make_grad_mixed(j):
            grad_hidden = mm(w3[j], block(1, j), 1, 0)
            grad_pre = (grad_hidden * slope[j]).astype(bf16)
            gpre[j] = grad_pre
            return mm(w2[j], grad_pre, 1, 0)

        @pl.when(is_last)
        def _():
            gbuf[...] = cot_ref[...]
            produce(1, make_grad_last)
            send(1)

        produce(0, make_first)
        send(0)
        arrive(0)

        def forward(j, carry):
            pre = mm(w2[j], block(0, j), 0, 0)
            cumulative = 0.5 * (1.0 + lax.erf(pre * root_half))
            hidden[j] = (pre * cumulative).astype(bf16)
            slope[j] = cumulative + pre * jnp.exp(-0.5 * pre * pre) * norm_density
            return carry

        lax.fori_loop(0, lb, forward, 0)

        @pl.when(not_last)
        def _():
            produce(2, make_down)
            send(2)
            hand_on().wait_recv()
            produce(1, make_grad_last)
            send(1)

        arrive(1)
        produce(3, make_grad_mixed)
        send(3)

        @pl.when(is_last)
        def _():
            produce(2, make_down)
            send(2)

        def grad_second(j, carry):
            value = mm(block(0, j), gpre[j], 1, 1) * factor
            st2[:, j] = value.astype(bf16).reshape(nd, bs // nd, hb)
            return carry

        def grad_down(j, carry):
            value = mm(hidden[j], block(1, j), 1, 1) * factor
            st3[:, j] = value.astype(bf16).reshape(nd, hb // nd, bs)
            return carry

        lax.fori_loop(0, lb, grad_second, 0)
        spread(1)
        lax.fori_loop(0, lb, grad_down, 0)
        spread(2)

        arrive(3)

        def outgoing(i, carry):
            acts = mm(w1[i], block(3, i), 1, 0).T
            gout[:, cols(i)] = (gbuf[:, cols(i)].astype(f32) + acts).astype(bf16)
            return carry

        lax.fori_loop(0, lb, outgoing, 0)

        @pl.when(not_first)
        def _():
            hand_on().start()

        def grad_first(i, carry):
            value = mm(x_ref[:, cols(i)].T, block(3, i), 1, 1) * factor
            st1[:, i] = value.astype(bf16).reshape(nd, bs // nd, bs)
            return carry

        lax.fori_loop(0, lb, grad_first, 0)
        spread(0)
        arrive(2)

        def grad_last(i, carry):
            value = mm(block(2, i), gbuf[:, cols(i)], 1, 0) * factor
            st4[:, i] = value.astype(bf16).reshape(nd, bs // nd, bs)
            return carry

        lax.fori_loop(0, lb, grad_last, 0)
        spread(3)

        for which in range(4):
            for k in range(1, nt):
                a2a(which, k).wait_send()
        for which in range(4):
            own(which).wait()
            for k in range(1, nd):
                share(which, k).wait()

        @pl.when(not_first)
        def _():
            hand_on().wait_send()

    return kernel


def body(inputs, cotangent, up_first, up_second, down_first, down_second):
    nt, nd, ns = (lax.axis_size(a) for a in ("tensor", "dp", "pipe"))
    tokens, width = cotangent.shape
    lb, bs, hb = up_second.shape[1:]
    tp = -(-tokens // lanes) * lanes
    factor = 1.0 / math.sqrt(tokens * nd)
    pad = ((0, tp - tokens), (0, 0))
    vmem = pl.BlockSpec(memory_space=pltpu.VMEM)
    anywhere = pl.BlockSpec(memory_space=pl.ANY)
    shapes = (
        (nd, lb, bs // nd, bs),
        (nd, lb, bs // nd, hb),
        (nd, lb, hb // nd, bs),
        (nd, lb, bs // nd, bs),
    )
    stride = bs // (nt * lb)
    exchange = (4, nt, lb, lb * stride, tp)
    dma = pltpu.SemaphoreType.DMA
    flops = 2 * tp * lb * bs * (8 * bs + 10 * hb)
    out = pl.pallas_call(
        make_kernel((nt, nd, ns, lb, bs, hb, tp), factor),
        out_shape=(jax.ShapeDtypeStruct((tp, width), bf16),)
        + tuple(jax.ShapeDtypeStruct(s, bf16) for s in shapes),
        in_specs=[vmem] * 6,
        out_specs=(vmem,) + (anywhere,) * 4,
        scratch_shapes=[
            pltpu.VMEM((tp, width), bf16),
            pltpu.VMEM(exchange, bf16),
            pltpu.VMEM(exchange, bf16),
            pltpu.VMEM((lb, hb, tp), bf16),
            pltpu.VMEM((lb, hb, tp), f32),
            pltpu.VMEM((lb, hb, tp), bf16),
        ]
        + [pltpu.VMEM(s, bf16) for s in shapes]
        + [
            dma((4, nt)),
            dma((4, nt)),
            dma((4, nd)),
            dma((4, nd)),
            dma((4,)),
            dma,
            dma,
        ],
        compiler_params=pltpu.CompilerParams(
            collective_id=0, has_side_effects=True, vmem_limit_bytes=60 * 1024 * 1024
        ),
        cost_estimate=pl.CostEstimate(
            flops=flops, bytes_accessed=8 * lb * bs * hb, transcendentals=2 * lb * hb * tp
        ),
    )(
        jnp.pad(inputs[0], pad),
        jnp.pad(cotangent, pad),
        up_first[0],
        up_second[0],
        down_first[0],
        down_second[0],
    )
    sums = tuple(jnp.sum(part.astype(f32), axis=0)[None] for part in out[1:])
    return (out[0][None, :tokens],) + sums


def solution(mesh):
    return jax.shard_map(
        body,
        mesh=mesh,
        in_specs=(
            P("pipe", "dp", "tensor"),
            P("dp", "tensor"),
            P("pipe", "tensor", None, None),
            P("pipe", "tensor", None, None),
            P("pipe", "tensor", None, None),
            P("pipe", "tensor", None, None),
        ),
        out_specs=(
            P("pipe", "dp", "tensor"),
            P("pipe", "tensor", "dp", None),
            P("pipe", "tensor", "dp", None),
            P("pipe", "tensor", "dp", None),
            P("pipe", "tensor", "dp", None),
        ),
        check_vma=False,
    )
```

```python
import math

import jax
import jax.numpy as jnp
from jax import lax
from jax.experimental import pallas as pl
from jax.experimental.pallas import tpu as pltpu
from jax.sharding import PartitionSpec as P

MESH = pl.DeviceIdType.MESH
root_half = 1.0 / math.sqrt(2.0)
norm_density = 1.0 / math.sqrt(2.0 * math.pi)
lanes = 128
f32 = jnp.float32
bf16 = jnp.bfloat16


def mm(left, right, left_dim, right_dim):
    return lax.dot_general(
        left, right, (((left_dim,), (right_dim,)), ((), ())), preferred_element_type=f32
    )


def make_token_kernel(sizes, factor):
    nt, nd, ns, lb, bs, hb, tp = sizes
    stride = bs // (nt * lb)
    rows = lb * stride

    def kernel(
        x_ref, cot_ref, w1, w2, w3, w4,
        gout, r1, r2, r3, r4,
        gbuf, sbuf, rbuf, hidden, slope, gpre, st1, st2, st3, st4,
        a_send, a_recv, d_send, d_recv, own_sem, p_send, p_recv,
    ):
        me_t = lax.axis_index("tensor")
        me_d = lax.axis_index("dp")
        me_s = lax.axis_index("pipe")
        is_last = me_s == ns - 1
        not_last = me_s < ns - 1
        not_first = me_s > 0

        barrier = pltpu.get_barrier_semaphore()
        for k in range(1, nt):
            pl.semaphore_signal(
                barrier, inc=1, device_id={"tensor": lax.rem(me_t + k, nt)}, device_id_type=MESH
            )
        for k in range(1, nd):
            pl.semaphore_signal(
                barrier, inc=1, device_id={"dp": lax.rem(me_d + k, nd)}, device_id_type=MESH
            )

        for k in range(1, ns):
            pl.semaphore_signal(
                barrier, inc=1, device_id={"pipe": lax.rem(me_s + k, ns)}, device_id_type=MESH
            )
        pl.semaphore_wait(barrier, nt - 1 + nd - 1 + ns - 1)

        def cols(i):
            return pl.ds(pl.multiple_of(i * bs, bs), bs)

        def produce(which, make):
            def pair(p, carry):
                parts = [make(2 * p + u).reshape(nt, lb, stride, tp) for u in range(2)]
                both = jnp.concatenate(parts, axis=2).astype(bf16)
                at = pl.multiple_of(p * 2 * stride, 2 * stride)
                sbuf[which, :, :, pl.ds(at, 2 * stride), :] = both
                return carry

            lax.fori_loop(0, lb // 2, pair, 0)

        def a2a(which, k):
            peer = lax.rem(me_t + k, nt)
            return pltpu.make_async_remote_copy(
                src_ref=sbuf.at[which, peer],
                dst_ref=rbuf.at[which, me_t],
                send_sem=a_send.at[which, k],
                recv_sem=a_recv.at[which, k],
                device_id={"tensor": peer},
                device_id_type=MESH,
            )

        def send(which):
            for k in range(1, nt):
                a2a(which, k).start()
            rbuf[which, me_t] = sbuf[which, me_t]

        def arrive(which):
            for k in range(1, nt):
                a2a(which, k).wait_recv()

        def block(which, j):
            return rbuf[which, :, j].reshape(bs, tp)

        pairs = ((st1, r1), (st2, r2), (st3, r3), (st4, r4))

        def share(which, k):
            staged, landed = pairs[which]
            peer = lax.rem(me_d + k, nd)
            return pltpu.make_async_remote_copy(
                src_ref=staged.at[peer],
                dst_ref=landed.at[me_d],
                send_sem=d_send.at[which, k],
                recv_sem=d_recv.at[which, k],
                device_id={"dp": peer},
                device_id_type=MESH,
            )

        def own(which):
            staged, landed = pairs[which]
            return pltpu.make_async_copy(staged.at[me_d], landed.at[me_d], own_sem.at[which])

        def spread(which):
            for k in range(1, nd):
                share(which, k).start()
            own(which).start()

        def hand_on():
            return pltpu.make_async_remote_copy(
                src_ref=gout,
                dst_ref=gbuf,
                send_sem=p_send,
                recv_sem=p_recv,
                device_id={"pipe": lax.rem(me_s + ns - 1, ns)},
                device_id_type=MESH,
            )

        def make_first(i):
            return mm(w1[i], x_ref[:, cols(i)], 0, 1)

        def make_grad_last(i):
            return mm(w4[i], gbuf[:, cols(i)], 1, 1)

        def make_down(j):
            return mm(w3[j], hidden[j], 0, 0)

        def make_grad_mixed(j):
            grad_hidden = mm(w3[j], block(1, j), 1, 0)
            grad_pre = (grad_hidden * slope[j]).astype(bf16)
            gpre[j] = grad_pre
            return mm(w2[j], grad_pre, 1, 0)

        @pl.when(is_last)
        def _():
            gbuf[...] = cot_ref[...]
            produce(1, make_grad_last)
            send(1)

        produce(0, make_first)
        send(0)
        arrive(0)

        def forward(j, carry):
            pre = mm(w2[j], block(0, j), 0, 0)
            cumulative = 0.5 * (1.0 + lax.erf(pre * root_half))
            hidden[j] = (pre * cumulative).astype(bf16)
            slope[j] = cumulative + pre * jnp.exp(-0.5 * pre * pre) * norm_density
            return carry

        lax.fori_loop(0, lb, forward, 0)

        @pl.when(not_last)
        def _():
            produce(2, make_down)
            send(2)
            hand_on().wait_recv()
            produce(1, make_grad_last)
            send(1)

        arrive(1)
        produce(3, make_grad_mixed)
        send(3)

        @pl.when(is_last)
        def _():
            produce(2, make_down)
            send(2)

        def grad_second(j, carry):
            value = mm(block(0, j), gpre[j], 1, 1) * factor
            st2[:, j] = value.astype(bf16).reshape(nd, bs // nd, hb)
            return carry

        def grad_down(j, carry):
            value = mm(hidden[j], block(1, j), 1, 1) * factor
            st3[:, j] = value.astype(bf16).reshape(nd, hb // nd, bs)
            return carry

        lax.fori_loop(0, lb, grad_second, 0)
        spread(1)
        lax.fori_loop(0, lb, grad_down, 0)
        spread(2)

        arrive(3)

        def outgoing(i, carry):
            acts = mm(w1[i], block(3, i), 1, 0).T
            gout[:, cols(i)] = (gbuf[:, cols(i)].astype(f32) + acts).astype(bf16)
            return carry

        lax.fori_loop(0, lb, outgoing, 0)

        @pl.when(not_first)
        def _():
            hand_on().start()

        def grad_first(i, carry):
            value = mm(x_ref[:, cols(i)].T, block(3, i), 1, 1) * factor
            st1[:, i] = value.astype(bf16).reshape(nd, bs // nd, bs)
            return carry

        lax.fori_loop(0, lb, grad_first, 0)
        spread(0)
        arrive(2)

        def grad_last(i, carry):
            value = mm(block(2, i), gbuf[:, cols(i)], 1, 0) * factor
            st4[:, i] = value.astype(bf16).reshape(nd, bs // nd, bs)
            return carry

        lax.fori_loop(0, lb, grad_last, 0)
        spread(3)

        for which in range(4):
            for k in range(1, nt):
                a2a(which, k).wait_send()
        for which in range(4):
            own(which).wait()
            for k in range(1, nd):
                share(which, k).wait()

        @pl.when(not_first)
        def _():
            hand_on().wait_send()

    return kernel


def tokens_split(inputs, cotangent, up_first, up_second, down_first, down_second):
    nt, nd, ns = (lax.axis_size(a) for a in ("tensor", "dp", "pipe"))
    tokens, width = cotangent.shape
    lb, bs, hb = up_second.shape[1:]
    tp = -(-tokens // lanes) * lanes
    factor = 1.0 / math.sqrt(tokens * nd)
    pad = ((0, tp - tokens), (0, 0))
    vmem = pl.BlockSpec(memory_space=pltpu.VMEM)
    anywhere = pl.BlockSpec(memory_space=pl.ANY)
    shapes = (
        (nd, lb, bs // nd, bs),
        (nd, lb, bs // nd, hb),
        (nd, lb, hb // nd, bs),
        (nd, lb, bs // nd, bs),
    )
    stride = bs // (nt * lb)
    exchange = (4, nt, lb, lb * stride, tp)
    dma = pltpu.SemaphoreType.DMA
    flops = 2 * tp * lb * bs * (8 * bs + 10 * hb)
    out = pl.pallas_call(
        make_token_kernel((nt, nd, ns, lb, bs, hb, tp), factor),
        out_shape=(jax.ShapeDtypeStruct((tp, width), bf16),)
        + tuple(jax.ShapeDtypeStruct(s, bf16) for s in shapes),
        in_specs=[vmem] * 6,
        out_specs=(vmem,) + (anywhere,) * 4,
        scratch_shapes=[
            pltpu.VMEM((tp, width), bf16),
            pltpu.VMEM(exchange, bf16),
            pltpu.VMEM(exchange, bf16),
            pltpu.VMEM((lb, hb, tp), bf16),
            pltpu.VMEM((lb, hb, tp), f32),
            pltpu.VMEM((lb, hb, tp), bf16),
        ]
        + [pltpu.VMEM(s, bf16) for s in shapes]
        + [
            dma((4, nt)),
            dma((4, nt)),
            dma((4, nd)),
            dma((4, nd)),
            dma((4,)),
            dma,
            dma,
        ],
        compiler_params=pltpu.CompilerParams(
            collective_id=0, has_side_effects=True, vmem_limit_bytes=60 * 1024 * 1024
        ),
        cost_estimate=pl.CostEstimate(
            flops=flops, bytes_accessed=8 * lb * bs * hb, transcendentals=2 * lb * hb * tp
        ),
    )(
        jnp.pad(inputs[0], pad),
        jnp.pad(cotangent, pad),
        up_first[0],
        up_second[0],
        down_first[0],
        down_second[0],
    )
    sums = tuple(jnp.sum(part.astype(f32), axis=0)[None] for part in out[1:])
    return (out[0][None, :tokens],) + sums


def make_block_kernel(sizes, factor):
    nt, nd, ns, nb, bs, hb, tokens = sizes
    group = nt * nd
    stride = bs // (group * nb)
    rows = nb * stride
    total = nd * tokens
    wide = nb * bs
    pieces = hb // bs

    def kernel(
        x_hbm, cot_hbm, h1, h2, h3, h4,
        gout, r1, r2, r3, r4,
        xbuf, gbuf, obuf, w1, w2, w3, w4,
        sbuf, rbuf, hidden, slope, gpre, st1, st2, st3, st4,
        w_sem, a_send, a_recv, d_send, d_recv, own_sem, p_send, p_recv, go,
    ):
        me_t = lax.axis_index("tensor")
        me_d = lax.axis_index("dp")
        me_s = lax.axis_index("pipe")
        me = me_t * nd + me_d
        is_last = me_s == ns - 1
        not_last = me_s < ns - 1
        not_first = me_s > 0

        def loop(start, stop, step):
            def run(k, carry):
                step(k)
                return carry

            lax.fori_loop(start, stop, run, 0)

        mine = pl.ds(me_d * nb, nb)
        loads = [
            pltpu.make_async_copy(source.at[mine], held, w_sem.at[n])
            for n, (source, held) in enumerate(((h1, w1), (h2, w2), (h3, w3), (h4, w4)))
        ]
        for n in (3, 0, 1, 2):
            loads[n].start()

        def member(k):
            peer = lax.rem(me + k, group)
            return peer, {"tensor": lax.div(peer, nd), "dp": lax.rem(peer, nd)}

        barrier = pltpu.get_barrier_semaphore()

        def greet(k):
            pl.semaphore_signal(barrier, inc=1, device_id=member(k)[1], device_id_type=MESH)

        loop(1, group, greet)
        for k in range(1, ns):
            pl.semaphore_signal(
                barrier, inc=1, device_id={"pipe": lax.rem(me_s + k, ns)}, device_id_type=MESH
            )
        pl.semaphore_wait(barrier, group - 1 + ns - 1)

        def wide_cols(d):
            return pl.ds(pl.multiple_of(d * wide, wide), wide)

        def cols(u):
            return pl.ds(u * bs, bs)

        def source_of(which, d):
            if which == 0:
                return x_hbm.at[:, wide_cols(d)]
            if which == 1:
                return cot_hbm.at[:, wide_cols(d)]
            return (st1, st2, st3, st4, obuf)[which - 2].at[d]

        def target_of(which):
            if which == 6:
                return gout.at[:, wide_cols(me_d)]
            return (xbuf, gbuf, r1, r2, r3, r4)[which].at[me_d]

        def share(which, k):
            peer = lax.rem(me_d + k, nd)
            return pltpu.make_async_remote_copy(
                src_ref=source_of(which, peer),
                dst_ref=target_of(which),
                send_sem=d_send.at[which, k],
                recv_sem=d_recv.at[which, k],
                device_id={"dp": peer},
                device_id_type=MESH,
            )

        def own(which):
            return pltpu.make_async_copy(
                source_of(which, me_d), target_of(which), own_sem.at[which]
            )

        def spread(which):
            for k in range(1, nd):
                share(which, k).start()
            own(which).start()

        def gathered(which):
            own(which).wait()
            for k in range(1, nd):
                share(which, k).wait_recv()

        def a2a(which, k):
            peer, where = member(k)
            return pltpu.make_async_remote_copy(
                src_ref=sbuf.at[which, peer],
                dst_ref=rbuf.at[which, me],
                send_sem=a_send.at[which, k],
                recv_sem=a_recv.at[which, k],
                device_id=where,
                device_id_type=MESH,
            )

        def send(which):
            loop(1, group, lambda k: a2a(which, k).start())
            rbuf[which, me] = sbuf[which, me]

        def arrive(which):
            loop(1, group, lambda k: a2a(which, k).wait_recv())

        def produce(which, make):
            parts = [make(u).reshape(group, nb, stride, total) for u in range(nb)]
            sbuf[which] = jnp.concatenate(parts, axis=2).astype(bf16)

        def block(which, j):
            return rbuf[which, :, j].reshape(bs, total)

        def tokens_of(ref, u):
            return ref[:, :, cols(u)].reshape(total, bs)

        def hand_on():
            return pltpu.make_async_remote_copy(
                src_ref=obuf,
                dst_ref=gbuf,
                send_sem=p_send,
                recv_sem=p_recv,
                device_id={"pipe": lax.rem(me_s + ns - 1, ns)},
                device_id_type=MESH,
            )

        def make_first(u):
            return mm(w1[u], tokens_of(xbuf, u), 0, 1)

        def make_grad_last(u):
            return mm(w4[u], tokens_of(gbuf, u), 1, 1)

        def make_down(u):
            return mm(w3[u], hidden[u], 0, 0)

        def make_grad_mixed(u):
            return mm(w2[u], gpre[u], 1, 0)

        def piece(n):
            return lax.div(n, pieces), pl.ds(pl.multiple_of(lax.rem(n, pieces) * bs, bs), bs)

        @pl.when(is_last)
        def _():
            spread(1)

        spread(0)
        loads[3].wait()
        loads[0].wait()

        @pl.when(is_last)
        def _():
            gathered(1)
            produce(1, make_grad_last)
            send(1)

        gathered(0)
        produce(0, make_first)

        @pl.when(not_last)
        def _():
            pl.semaphore_wait(go, 1)

        send(0)
        loads[1].wait()
        loads[2].wait()
        arrive(0)

        @pl.when(not_first)
        def _():
            pl.semaphore_signal(go, inc=1, device_id={"pipe": me_s - 1}, device_id_type=MESH)

        def forward(n):
            u, part = piece(n)
            pre = mm(w2[u, :, part], block(0, u), 0, 0)
            cumulative = 0.5 * (1.0 + lax.erf(pre * root_half))
            hidden[u, part] = (pre * cumulative).astype(bf16)
            slope[u, part] = cumulative + pre * jnp.exp(-0.5 * pre * pre) * norm_density

        loop(0, nb * pieces, forward)

        @pl.when(not_last)
        def _():
            produce(2, make_down)
            send(2)
            hand_on().wait_recv()
            produce(1, make_grad_last)
            send(1)

        arrive(1)

        def backward(n):
            u, part = piece(n)
            gpre[u, part] = (mm(w3[u, part], block(1, u), 1, 0) * slope[u, part]).astype(bf16)

        loop(0, nb * pieces, backward)
        produce(3, make_grad_mixed)
        send(3)

        @pl.when(is_last)
        def _():
            produce(2, make_down)
            send(2)

        def scaled(value, out_rows):
            return (value * factor).astype(bf16).reshape(nd, out_rows // nd, value.shape[1])

        for u in range(nb):
            st2[:, u] = scaled(mm(block(0, u), gpre[u], 1, 1), bs)
        spread(3)
        for u in range(nb):
            st3[:, u] = scaled(mm(hidden[u], block(1, u), 1, 1), hb)
        spread(4)

        arrive(3)
        for u in range(nb):
            acts = mm(block(3, u), w1[u], 0, 1)
            fresh = tokens_of(gbuf, u).astype(f32) + acts
            obuf[:, :, cols(u)] = fresh.astype(bf16).reshape(nd, tokens, bs)

        @pl.when(not_first)
        def _():
            hand_on().start()

        spread(6)
        for u in range(nb):
            st1[:, u] = scaled(mm(tokens_of(xbuf, u).T, block(3, u), 1, 1), bs)
        spread(2)
        arrive(2)
        for u in range(nb):
            st4[:, u] = scaled(mm(block(2, u), tokens_of(gbuf, u), 1, 0), bs)
        spread(5)

        for which in range(4):
            loop(1, group, lambda k: a2a(which, k).wait_send())
        for k in range(1, nd):
            share(0, k).wait_send()

        @pl.when(is_last)
        def _():
            for k in range(1, nd):
                share(1, k).wait_send()

        for which in range(2, 7):
            own(which).wait()
            for k in range(1, nd):
                share(which, k).wait()

        @pl.when(not_first)
        def _():
            hand_on().wait_send()

    return kernel


def blocks_split(inputs, cotangent, up_first, up_second, down_first, down_second):
    nt, nd, ns = (lax.axis_size(a) for a in ("tensor", "dp", "pipe"))
    tokens, width = cotangent.shape
    lb, bs, hb = up_second.shape[1:]
    nb = lb // nd
    total = nd * tokens
    factor = 1.0 / math.sqrt(total)
    anywhere = pl.BlockSpec(memory_space=pl.ANY)
    shapes = (
        (nd, nb, bs // nd, bs),
        (nd, nb, bs // nd, hb),
        (nd, nb, hb // nd, bs),
        (nd, nb, bs // nd, bs),
    )
    group = nt * nd
    exchange = (4, group, nb, bs // group, total)
    dma = pltpu.SemaphoreType.DMA
    flops = 2 * total * nb * bs * (8 * bs + 10 * hb)
    out = pl.pallas_call(
        make_block_kernel((nt, nd, ns, nb, bs, hb, tokens), factor),
        out_shape=(jax.ShapeDtypeStruct((tokens, width), bf16),)
        + tuple(jax.ShapeDtypeStruct(s, bf16) for s in shapes),
        in_specs=[anywhere] * 6,
        out_specs=(anywhere,) * 5,
        scratch_shapes=[pltpu.VMEM((nd, tokens, nb * bs), bf16)] * 3
        + [
            pltpu.VMEM((nb, bs, bs), bf16),
            pltpu.VMEM((nb, bs, hb), bf16),
            pltpu.VMEM((nb, hb, bs), bf16),
            pltpu.VMEM((nb, bs, bs), bf16),
            pltpu.VMEM(exchange, bf16),
            pltpu.VMEM(exchange, bf16),
            pltpu.VMEM((nb, hb, total), bf16),
            pltpu.VMEM((nb, hb, total), f32),
            pltpu.VMEM((nb, hb, total), bf16),
        ]
        + [pltpu.VMEM(s, bf16) for s in shapes]
        + [
            dma((4,)),
            dma((4, group)),
            dma((4, group)),
            dma((7, nd)),
            dma((7, nd)),
            dma((7,)),
            dma,
            dma,
            pltpu.SemaphoreType.REGULAR,
        ],
        compiler_params=pltpu.CompilerParams(
            collective_id=1, has_side_effects=True, vmem_limit_bytes=60 * 1024 * 1024
        ),
        cost_estimate=pl.CostEstimate(
            flops=flops, bytes_accessed=8 * lb * bs * hb, transcendentals=2 * nb * hb * total
        ),
    )(inputs[0], cotangent, up_first[0], up_second[0], down_first[0], down_second[0])
    grads = tuple(
        part.reshape((lb,) + part.shape[2:]).astype(f32)[None] for part in out[1:]
    )
    return (out[0][None],) + grads


def body(inputs, cotangent, up_first, up_second, down_first, down_second):
    arrays = (inputs, cotangent, up_first, up_second, down_first, down_second)
    nd = lax.axis_size("dp")
    tokens = cotangent.shape[0]
    stride = up_first.shape[-1] // (up_first.shape[1] * lax.axis_size("tensor"))
    nb = up_first.shape[1] // nd
    divides = up_first.shape[1] % nd == 0 and nb * stride % 16 == 0 and nb > 0
    if divides and tokens % 16 == 0 and tokens * nd % lanes == 0:
        return blocks_split(*arrays)
    return tokens_split(*arrays)


def solution(mesh):
    return jax.shard_map(
        body,
        mesh=mesh,
        in_specs=(
            P("pipe", "dp", "tensor"),
            P("dp", "tensor"),
            P("pipe", "tensor", None, None),
            P("pipe", "tensor", None, None),
            P("pipe", "tensor", None, None),
            P("pipe", "tensor", None, None),
        ),
        out_specs=(
            P("pipe", "dp", "tensor"),
            P("pipe", "tensor", "dp", None),
            P("pipe", "tensor", "dp", None),
            P("pipe", "tensor", "dp", None),
            P("pipe", "tensor", "dp", None),
        ),
        check_vma=False,
    )
```

```python
import math

import jax
import jax.numpy as jnp
from jax import lax
from jax.experimental import pallas as pl
from jax.experimental.pallas import tpu as pltpu
from jax.sharding import PartitionSpec as P

MESH = pl.DeviceIdType.MESH
root_half = 1.0 / math.sqrt(2.0)
norm_density = 1.0 / math.sqrt(2.0 * math.pi)
lanes = 128
f32 = jnp.float32
bf16 = jnp.bfloat16


def mm(left, right, left_dim, right_dim):
    return lax.dot_general(
        left, right, (((left_dim,), (right_dim,)), ((), ())), preferred_element_type=f32
    )


def make_token_kernel(sizes, factor):
    nt, nd, ns, lb, bs, hb, tp = sizes
    stride = bs // (nt * lb)
    rows = lb * stride

    def kernel(
        x_ref, cot_ref, w1, w2, w3, w4,
        gout, r1, r2, r3, r4,
        gbuf, sbuf, rbuf, hidden, slope, gpre, st1, st2, st3, st4,
        a_send, a_recv, d_send, d_recv, own_sem, p_send, p_recv,
    ):
        me_t = lax.axis_index("tensor")
        me_d = lax.axis_index("dp")
        me_s = lax.axis_index("pipe")
        is_last = me_s == ns - 1
        not_last = me_s < ns - 1
        not_first = me_s > 0

        barrier = pltpu.get_barrier_semaphore()
        for k in range(1, nt):
            pl.semaphore_signal(
                barrier, inc=1, device_id={"tensor": lax.rem(me_t + k, nt)}, device_id_type=MESH
            )
        for k in range(1, nd):
            pl.semaphore_signal(
                barrier, inc=1, device_id={"dp": lax.rem(me_d + k, nd)}, device_id_type=MESH
            )

        for k in range(1, ns):
            pl.semaphore_signal(
                barrier, inc=1, device_id={"pipe": lax.rem(me_s + k, ns)}, device_id_type=MESH
            )
        pl.semaphore_wait(barrier, nt - 1 + nd - 1 + ns - 1)

        def cols(i):
            return pl.ds(pl.multiple_of(i * bs, bs), bs)

        def produce(which, make):
            def pair(p, carry):
                parts = [make(2 * p + u).reshape(nt, lb, stride, tp) for u in range(2)]
                both = jnp.concatenate(parts, axis=2).astype(bf16)
                at = pl.multiple_of(p * 2 * stride, 2 * stride)
                sbuf[which, :, :, pl.ds(at, 2 * stride), :] = both
                return carry

            lax.fori_loop(0, lb // 2, pair, 0)

        def a2a(which, k):
            peer = lax.rem(me_t + k, nt)
            return pltpu.make_async_remote_copy(
                src_ref=sbuf.at[which, peer],
                dst_ref=rbuf.at[which, me_t],
                send_sem=a_send.at[which, k],
                recv_sem=a_recv.at[which, k],
                device_id={"tensor": peer},
                device_id_type=MESH,
            )

        def send(which):
            for k in range(1, nt):
                a2a(which, k).start()
            rbuf[which, me_t] = sbuf[which, me_t]

        def arrive(which):
            for k in range(1, nt):
                a2a(which, k).wait_recv()

        def block(which, j):
            return rbuf[which, :, j].reshape(bs, tp)

        pairs = ((st1, r1), (st2, r2), (st3, r3), (st4, r4))

        def share(which, k):
            staged, landed = pairs[which]
            peer = lax.rem(me_d + k, nd)
            return pltpu.make_async_remote_copy(
                src_ref=staged.at[peer],
                dst_ref=landed.at[me_d],
                send_sem=d_send.at[which, k],
                recv_sem=d_recv.at[which, k],
                device_id={"dp": peer},
                device_id_type=MESH,
            )

        def own(which):
            staged, landed = pairs[which]
            return pltpu.make_async_copy(staged.at[me_d], landed.at[me_d], own_sem.at[which])

        def spread(which):
            for k in range(1, nd):
                share(which, k).start()
            own(which).start()

        def hand_on():
            return pltpu.make_async_remote_copy(
                src_ref=gout,
                dst_ref=gbuf,
                send_sem=p_send,
                recv_sem=p_recv,
                device_id={"pipe": lax.rem(me_s + ns - 1, ns)},
                device_id_type=MESH,
            )

        def make_first(i):
            return mm(w1[i], x_ref[:, cols(i)], 0, 1)

        def make_grad_last(i):
            return mm(w4[i], gbuf[:, cols(i)], 1, 1)

        def make_down(j):
            return mm(w3[j], hidden[j], 0, 0)

        def make_grad_mixed(j):
            grad_hidden = mm(w3[j], block(1, j), 1, 0)
            grad_pre = (grad_hidden * slope[j]).astype(bf16)
            gpre[j] = grad_pre
            return mm(w2[j], grad_pre, 1, 0)

        @pl.when(is_last)
        def _():
            gbuf[...] = cot_ref[...]
            produce(1, make_grad_last)
            send(1)

        produce(0, make_first)
        send(0)
        arrive(0)

        def forward(j, carry):
            pre = mm(w2[j], block(0, j), 0, 0)
            cumulative = 0.5 * (1.0 + lax.erf(pre * root_half))
            hidden[j] = (pre * cumulative).astype(bf16)
            slope[j] = cumulative + pre * jnp.exp(-0.5 * pre * pre) * norm_density
            return carry

        lax.fori_loop(0, lb, forward, 0)

        @pl.when(not_last)
        def _():
            produce(2, make_down)
            send(2)
            hand_on().wait_recv()
            produce(1, make_grad_last)
            send(1)

        arrive(1)
        produce(3, make_grad_mixed)
        send(3)

        @pl.when(is_last)
        def _():
            produce(2, make_down)
            send(2)

        def grad_second(j, carry):
            value = mm(block(0, j), gpre[j], 1, 1) * factor
            st2[:, j] = value.astype(bf16).reshape(nd, bs // nd, hb)
            return carry

        def grad_down(j, carry):
            value = mm(hidden[j], block(1, j), 1, 1) * factor
            st3[:, j] = value.astype(bf16).reshape(nd, hb // nd, bs)
            return carry

        lax.fori_loop(0, lb, grad_second, 0)
        spread(1)
        lax.fori_loop(0, lb, grad_down, 0)
        spread(2)

        arrive(3)

        def outgoing(i, carry):
            acts = mm(w1[i], block(3, i), 1, 0).T
            gout[:, cols(i)] = (gbuf[:, cols(i)].astype(f32) + acts).astype(bf16)
            return carry

        lax.fori_loop(0, lb, outgoing, 0)

        @pl.when(not_first)
        def _():
            hand_on().start()

        def grad_first(i, carry):
            value = mm(x_ref[:, cols(i)].T, block(3, i), 1, 1) * factor
            st1[:, i] = value.astype(bf16).reshape(nd, bs // nd, bs)
            return carry

        lax.fori_loop(0, lb, grad_first, 0)
        spread(0)
        arrive(2)

        def grad_last(i, carry):
            value = mm(block(2, i), gbuf[:, cols(i)], 1, 0) * factor
            st4[:, i] = value.astype(bf16).reshape(nd, bs // nd, bs)
            return carry

        lax.fori_loop(0, lb, grad_last, 0)
        spread(3)

        for which in range(4):
            for k in range(1, nt):
                a2a(which, k).wait_send()
        for which in range(4):
            own(which).wait()
            for k in range(1, nd):
                share(which, k).wait()

        @pl.when(not_first)
        def _():
            hand_on().wait_send()

    return kernel


def tokens_split(inputs, cotangent, up_first, up_second, down_first, down_second):
    nt, nd, ns = (lax.axis_size(a) for a in ("tensor", "dp", "pipe"))
    tokens, width = cotangent.shape
    lb, bs, hb = up_second.shape[1:]
    tp = -(-tokens // lanes) * lanes
    factor = 1.0 / math.sqrt(tokens * nd)
    pad = ((0, tp - tokens), (0, 0))
    vmem = pl.BlockSpec(memory_space=pltpu.VMEM)
    anywhere = pl.BlockSpec(memory_space=pl.ANY)
    shapes = (
        (nd, lb, bs // nd, bs),
        (nd, lb, bs // nd, hb),
        (nd, lb, hb // nd, bs),
        (nd, lb, bs // nd, bs),
    )
    stride = bs // (nt * lb)
    exchange = (4, nt, lb, lb * stride, tp)
    dma = pltpu.SemaphoreType.DMA
    flops = 2 * tp * lb * bs * (8 * bs + 10 * hb)
    out = pl.pallas_call(
        make_token_kernel((nt, nd, ns, lb, bs, hb, tp), factor),
        out_shape=(jax.ShapeDtypeStruct((tp, width), bf16),)
        + tuple(jax.ShapeDtypeStruct(s, bf16) for s in shapes),
        in_specs=[vmem] * 6,
        out_specs=(vmem,) + (anywhere,) * 4,
        scratch_shapes=[
            pltpu.VMEM((tp, width), bf16),
            pltpu.VMEM(exchange, bf16),
            pltpu.VMEM(exchange, bf16),
            pltpu.VMEM((lb, hb, tp), bf16),
            pltpu.VMEM((lb, hb, tp), f32),
            pltpu.VMEM((lb, hb, tp), bf16),
        ]
        + [pltpu.VMEM(s, bf16) for s in shapes]
        + [
            dma((4, nt)),
            dma((4, nt)),
            dma((4, nd)),
            dma((4, nd)),
            dma((4,)),
            dma,
            dma,
        ],
        compiler_params=pltpu.CompilerParams(
            collective_id=0, has_side_effects=True, vmem_limit_bytes=60 * 1024 * 1024
        ),
        cost_estimate=pl.CostEstimate(
            flops=flops, bytes_accessed=8 * lb * bs * hb, transcendentals=2 * lb * hb * tp
        ),
    )(
        jnp.pad(inputs[0], pad),
        jnp.pad(cotangent, pad),
        up_first[0],
        up_second[0],
        down_first[0],
        down_second[0],
    )
    sums = tuple(jnp.sum(part.astype(f32), axis=0)[None] for part in out[1:])
    return (out[0][None, :tokens],) + sums


def make_block_kernel(sizes, factor):
    nt, nd, ns, nb, bs, hb, tokens = sizes
    group = nt * nd
    stride = bs // (group * nb)
    rows = nb * stride
    total = nd * tokens
    wide = nb * bs
    pieces = hb // bs

    def kernel(
        x_hbm, cot_hbm, h1, h2, h3, h4,
        gout, r1, r2, r3, r4,
        xbuf, gbuf, obuf, w1, w2, w3, w4,
        sbuf, rbuf, hidden, slope, gpre, st1, st2, st3, st4,
        w_sem, a_send, a_recv, d_send, d_recv, own_sem, p_send, p_recv, go,
    ):
        me_t = lax.axis_index("tensor")
        me_d = lax.axis_index("dp")
        me_s = lax.axis_index("pipe")
        me = me_t * nd + me_d
        is_last = me_s == ns - 1
        not_last = me_s < ns - 1
        not_first = me_s > 0
        is_first = me_s == 0

        def loop(start, stop, step):
            def run(k, carry):
                step(k)
                return carry

            lax.fori_loop(start, stop, run, 0)

        mine = pl.ds(me_d * nb, nb)
        loads = [
            pltpu.make_async_copy(source.at[mine], held, w_sem.at[n])
            for n, (source, held) in enumerate(((h1, w1), (h2, w2), (h3, w3), (h4, w4)))
        ]
        for n in (0, 3, 1, 2):
            loads[n].start()

        def member(k):
            peer = lax.rem(me + k, group)
            return peer, {"tensor": lax.div(peer, nd), "dp": lax.rem(peer, nd)}

        barrier = pltpu.get_barrier_semaphore()

        def greet(k):
            pl.semaphore_signal(barrier, inc=1, device_id=member(k)[1], device_id_type=MESH)

        loop(1, group, greet)
        for k in range(1, ns):
            pl.semaphore_signal(
                barrier, inc=1, device_id={"pipe": lax.rem(me_s + k, ns)}, device_id_type=MESH
            )
        pl.semaphore_wait(barrier, group - 1 + ns - 1)

        def wide_cols(d):
            return pl.ds(pl.multiple_of(d * wide, wide), wide)

        def cols(u):
            return pl.ds(u * bs, bs)

        def source_of(which, d):
            if which == 0:
                return x_hbm.at[:, wide_cols(d)]
            if which == 1:
                return cot_hbm.at[:, wide_cols(d)]
            return (st1, st2, st3, st4, obuf)[which - 2].at[d]

        def target_of(which):
            if which == 6:
                return gout.at[:, wide_cols(me_d)]
            return (xbuf, gbuf, r1, r2, r3, r4)[which].at[me_d]

        def share(which, k):
            peer = lax.rem(me_d + k, nd)
            return pltpu.make_async_remote_copy(
                src_ref=source_of(which, peer),
                dst_ref=target_of(which),
                send_sem=d_send.at[which, k],
                recv_sem=d_recv.at[which, k],
                device_id={"dp": peer},
                device_id_type=MESH,
            )

        def own(which):
            return pltpu.make_async_copy(
                source_of(which, me_d), target_of(which), own_sem.at[which]
            )

        def spread(which):
            for k in range(1, nd):
                share(which, k).start()
            own(which).start()

        def gathered(which):
            own(which).wait()
            for k in range(1, nd):
                share(which, k).wait_recv()

        def a2a(which, k):
            peer, where = member(k)
            return pltpu.make_async_remote_copy(
                src_ref=sbuf.at[which, peer],
                dst_ref=rbuf.at[which, me],
                send_sem=a_send.at[which, k],
                recv_sem=a_recv.at[which, k],
                device_id=where,
                device_id_type=MESH,
            )

        def send(which):
            loop(1, group, lambda k: a2a(which, k).start())
            rbuf[which, me] = sbuf[which, me]

        def arrive(which):
            loop(1, group, lambda k: a2a(which, k).wait_recv())

        def produce(which, make):
            parts = [make(u).reshape(group, nb, stride, total) for u in range(nb)]
            sbuf[which] = jnp.concatenate(parts, axis=2).astype(bf16)

        def block(which, j):
            return rbuf[which, :, j].reshape(bs, total)

        def tokens_of(ref, u):
            return ref[:, :, cols(u)].reshape(total, bs)

        def hand_on():
            return pltpu.make_async_remote_copy(
                src_ref=obuf,
                dst_ref=gbuf,
                send_sem=p_send,
                recv_sem=p_recv,
                device_id={"pipe": lax.rem(me_s + ns - 1, ns)},
                device_id_type=MESH,
            )

        def make_first(u):
            return mm(w1[u], tokens_of(xbuf, u), 0, 1)

        def make_grad_last(u):
            return mm(w4[u], tokens_of(gbuf, u), 1, 1)

        def make_down(u):
            return mm(w3[u], hidden[u], 0, 0)

        def make_grad_mixed(u):
            return mm(w2[u], gpre[u], 1, 0)

        def piece(n):
            return lax.div(n, pieces), pl.ds(pl.multiple_of(lax.rem(n, pieces) * bs, bs), bs)

        def tell(which, step):
            pl.semaphore_signal(
                go.at[which], inc=1, device_id={"pipe": me_s + step}, device_id_type=MESH
            )

        def scaled(value, out_rows):
            return (value * factor).astype(bf16).reshape(nd, out_rows // nd, value.shape[1])

        def finish_first():
            for u in range(nb):
                st1[:, u] = scaled(mm(tokens_of(xbuf, u).T, block(3, u), 1, 1), bs)

        def finish_second():
            for u in range(nb):
                st2[:, u] = scaled(mm(block(0, u), gpre[u], 1, 1), bs)

        def finish_down():
            for u in range(nb):
                st3[:, u] = scaled(mm(hidden[u], block(1, u), 1, 1), hb)

        def finish_last():
            for u in range(nb):
                st4[:, u] = scaled(mm(block(2, u), tokens_of(gbuf, u), 1, 0), bs)

        @pl.when(not_last)
        def _():
            pl.semaphore_wait(go.at[0], 1)

        spread(0)

        @pl.when(is_last)
        def _():
            spread(1)

        loads[0].wait()
        gathered(0)
        produce(0, make_first)
        loads[3].wait()

        @pl.when(not_last)
        def _():
            pl.semaphore_wait(go.at[1], 1)

        send(0)

        @pl.when(is_last)
        def _():
            gathered(1)

        @pl.when(not_first)
        def _():
            tell(0, -1)

        @pl.when(is_last)
        def _():
            produce(1, make_grad_last)

        loads[1].wait()
        loads[2].wait()
        arrive(0)

        @pl.when(is_last)
        def _():
            send(1)

        def forward(n):
            u, part = piece(n)
            pre = mm(w2[u, :, part], block(0, u), 0, 0)
            cumulative = 0.5 * (1.0 + lax.erf(pre * root_half))
            hidden[u, part] = (pre * cumulative).astype(bf16)
            slope[u, part] = cumulative + pre * jnp.exp(-0.5 * pre * pre) * norm_density

        loop(0, nb * pieces, forward)

        @pl.when(not_last)
        def _():
            produce(2, make_down)
            pl.semaphore_wait(go.at[2], 1)
            send(2)
            hand_on().wait_recv()
            produce(1, make_grad_last)
            send(1)
            arrive(2)
            finish_last()
            spread(5)

        arrive(1)

        @pl.when(not_first)
        def _():
            tell(1, -1)

        @pl.when(not_last)
        def _():
            tell(3, 1)

        @pl.when(is_first)
        def _():
            finish_down()
            spread(4)

        def backward(n):
            u, part = piece(n)
            gpre[u, part] = (mm(w3[u, part], block(1, u), 1, 0) * slope[u, part]).astype(bf16)

        loop(0, nb * pieces, backward)
        produce(3, make_grad_mixed)
        send(3)
        finish_second()

        @pl.when(is_first)
        def _():
            spread(3)

        @pl.when(not_first)
        def _():
            finish_down()

        @pl.when(is_last)
        def _():
            produce(2, make_down)

        arrive(3)

        @pl.when(not_first)
        def _():
            tell(2, -1)

        for u in range(nb):
            acts = mm(block(3, u), w1[u], 0, 1)
            fresh = tokens_of(gbuf, u).astype(f32) + acts
            obuf[:, :, cols(u)] = fresh.astype(bf16).reshape(nd, tokens, bs)

        @pl.when(not_first)
        def _():
            hand_on().start()
            spread(3)
            spread(4)

        spread(6)
        finish_first()
        spread(2)

        @pl.when(not_first)
        def _():
            pl.semaphore_wait(go.at[3], 1)

        @pl.when(is_last)
        def _():
            send(2)
            arrive(2)
            finish_last()
            spread(5)

        for which in range(4):
            loop(1, group, lambda k: a2a(which, k).wait_send())
        for k in range(1, nd):
            share(0, k).wait_send()

        @pl.when(is_last)
        def _():
            for k in range(1, nd):
                share(1, k).wait_send()

        for which in range(2, 7):
            own(which).wait()
            for k in range(1, nd):
                share(which, k).wait()

        @pl.when(not_first)
        def _():
            hand_on().wait_send()

    return kernel


def blocks_split(inputs, cotangent, up_first, up_second, down_first, down_second):
    nt, nd, ns = (lax.axis_size(a) for a in ("tensor", "dp", "pipe"))
    tokens, width = cotangent.shape
    lb, bs, hb = up_second.shape[1:]
    nb = lb // nd
    total = nd * tokens
    factor = 1.0 / math.sqrt(total)
    anywhere = pl.BlockSpec(memory_space=pl.ANY)
    shapes = (
        (nd, nb, bs // nd, bs),
        (nd, nb, bs // nd, hb),
        (nd, nb, hb // nd, bs),
        (nd, nb, bs // nd, bs),
    )
    group = nt * nd
    exchange = (4, group, nb, bs // group, total)
    dma = pltpu.SemaphoreType.DMA
    flops = 2 * total * nb * bs * (8 * bs + 10 * hb)
    out = pl.pallas_call(
        make_block_kernel((nt, nd, ns, nb, bs, hb, tokens), factor),
        out_shape=(jax.ShapeDtypeStruct((tokens, width), bf16),)
        + tuple(jax.ShapeDtypeStruct(s, bf16) for s in shapes),
        in_specs=[anywhere] * 6,
        out_specs=(anywhere,) * 5,
        scratch_shapes=[pltpu.VMEM((nd, tokens, nb * bs), bf16)] * 3
        + [
            pltpu.VMEM((nb, bs, bs), bf16),
            pltpu.VMEM((nb, bs, hb), bf16),
            pltpu.VMEM((nb, hb, bs), bf16),
            pltpu.VMEM((nb, bs, bs), bf16),
            pltpu.VMEM(exchange, bf16),
            pltpu.VMEM(exchange, bf16),
            pltpu.VMEM((nb, hb, total), bf16),
            pltpu.VMEM((nb, hb, total), f32),
            pltpu.VMEM((nb, hb, total), bf16),
        ]
        + [pltpu.VMEM(s, bf16) for s in shapes]
        + [
            dma((4,)),
            dma((4, group)),
            dma((4, group)),
            dma((7, nd)),
            dma((7, nd)),
            dma((7,)),
            dma,
            dma,
            pltpu.SemaphoreType.REGULAR((4,)),
        ],
        compiler_params=pltpu.CompilerParams(
            collective_id=1, has_side_effects=True, vmem_limit_bytes=60 * 1024 * 1024
        ),
        cost_estimate=pl.CostEstimate(
            flops=flops, bytes_accessed=8 * lb * bs * hb, transcendentals=2 * nb * hb * total
        ),
    )(inputs[0], cotangent, up_first[0], up_second[0], down_first[0], down_second[0])
    grads = tuple(
        part.reshape((lb,) + part.shape[2:]).astype(f32)[None] for part in out[1:]
    )
    return (out[0][None],) + grads


def body(inputs, cotangent, up_first, up_second, down_first, down_second):
    arrays = (inputs, cotangent, up_first, up_second, down_first, down_second)
    nd = lax.axis_size("dp")
    tokens = cotangent.shape[0]
    stride = up_first.shape[-1] // (up_first.shape[1] * lax.axis_size("tensor"))
    nb = up_first.shape[1] // nd
    divides = up_first.shape[1] % nd == 0 and nb * stride % 16 == 0 and nb > 0
    if divides and tokens % 16 == 0 and tokens * nd % lanes == 0:
        return blocks_split(*arrays)
    return tokens_split(*arrays)


def solution(mesh):
    return jax.shard_map(
        body,
        mesh=mesh,
        in_specs=(
            P("pipe", "dp", "tensor"),
            P("dp", "tensor"),
            P("pipe", "tensor", None, None),
            P("pipe", "tensor", None, None),
            P("pipe", "tensor", None, None),
            P("pipe", "tensor", None, None),
        ),
        out_specs=(
            P("pipe", "dp", "tensor"),
            P("pipe", "tensor", "dp", None),
            P("pipe", "tensor", "dp", None),
            P("pipe", "tensor", "dp", None),
            P("pipe", "tensor", "dp", None),
        ),
        check_vma=False,
    )
```

```python
import math

import jax
import jax.numpy as jnp
from jax import lax
from jax.experimental import pallas as pl
from jax.experimental.pallas import tpu as pltpu
from jax.sharding import PartitionSpec as P

MESH = pl.DeviceIdType.MESH
root_half = 1.0 / math.sqrt(2.0)
norm_density = 1.0 / math.sqrt(2.0 * math.pi)
lanes = 128
tile = 16
f32 = jnp.float32
bf16 = jnp.bfloat16


def mm(left, right, left_dim, right_dim):
    return lax.dot_general(
        left, right, (((left_dim,), (right_dim,)), ((), ())), preferred_element_type=f32
    )


def make_token_kernel(sizes, factor):
    nt, nd, ns, lb, bs, hb, tp = sizes
    stride = bs // (nt * lb)
    rows = lb * stride

    def kernel(
        x_ref, cot_ref, w1, w2, w3, w4,
        gout, r1, r2, r3, r4,
        gbuf, sbuf, rbuf, hidden, slope, gpre, st1, st2, st3, st4,
        a_send, a_recv, d_send, d_recv, own_sem, p_send, p_recv,
    ):
        me_t = lax.axis_index("tensor")
        me_d = lax.axis_index("dp")
        me_s = lax.axis_index("pipe")
        is_last = me_s == ns - 1
        not_last = me_s < ns - 1
        not_first = me_s > 0

        barrier = pltpu.get_barrier_semaphore()
        for k in range(1, nt):
            pl.semaphore_signal(
                barrier, inc=1, device_id={"tensor": lax.rem(me_t + k, nt)}, device_id_type=MESH
            )
        for k in range(1, nd):
            pl.semaphore_signal(
                barrier, inc=1, device_id={"dp": lax.rem(me_d + k, nd)}, device_id_type=MESH
            )

        for k in range(1, ns):
            pl.semaphore_signal(
                barrier, inc=1, device_id={"pipe": lax.rem(me_s + k, ns)}, device_id_type=MESH
            )
        pl.semaphore_wait(barrier, nt - 1 + nd - 1 + ns - 1)

        def cols(i):
            return pl.ds(pl.multiple_of(i * bs, bs), bs)

        def produce(which, make):
            def pair(p, carry):
                parts = [make(2 * p + u).reshape(nt, lb, stride, tp) for u in range(2)]
                both = jnp.concatenate(parts, axis=2).astype(bf16)
                at = pl.multiple_of(p * 2 * stride, 2 * stride)
                sbuf[which, :, :, pl.ds(at, 2 * stride), :] = both
                return carry

            lax.fori_loop(0, lb // 2, pair, 0)

        def a2a(which, k):
            peer = lax.rem(me_t + k, nt)
            return pltpu.make_async_remote_copy(
                src_ref=sbuf.at[which, peer],
                dst_ref=rbuf.at[which, me_t],
                send_sem=a_send.at[which, k],
                recv_sem=a_recv.at[which, k],
                device_id={"tensor": peer},
                device_id_type=MESH,
            )

        def send(which):
            for k in range(1, nt):
                a2a(which, k).start()
            rbuf[which, me_t] = sbuf[which, me_t]

        def arrive(which):
            for k in range(1, nt):
                a2a(which, k).wait_recv()

        def block(which, j):
            return rbuf[which, :, j].reshape(bs, tp)

        pairs = ((st1, r1), (st2, r2), (st3, r3), (st4, r4))

        def share(which, k):
            staged, landed = pairs[which]
            peer = lax.rem(me_d + k, nd)
            return pltpu.make_async_remote_copy(
                src_ref=staged.at[peer],
                dst_ref=landed.at[me_d],
                send_sem=d_send.at[which, k],
                recv_sem=d_recv.at[which, k],
                device_id={"dp": peer},
                device_id_type=MESH,
            )

        def own(which):
            staged, landed = pairs[which]
            return pltpu.make_async_copy(staged.at[me_d], landed.at[me_d], own_sem.at[which])

        def spread(which):
            for k in range(1, nd):
                share(which, k).start()
            own(which).start()

        def hand_on():
            return pltpu.make_async_remote_copy(
                src_ref=gout,
                dst_ref=gbuf,
                send_sem=p_send,
                recv_sem=p_recv,
                device_id={"pipe": lax.rem(me_s + ns - 1, ns)},
                device_id_type=MESH,
            )

        def make_first(i):
            return mm(w1[i], x_ref[:, cols(i)], 0, 1)

        def make_grad_last(i):
            return mm(w4[i], gbuf[:, cols(i)], 1, 1)

        def make_down(j):
            return mm(w3[j], hidden[j], 0, 0)

        def make_grad_mixed(j):
            grad_hidden = mm(w3[j], block(1, j), 1, 0)
            grad_pre = (grad_hidden * slope[j]).astype(bf16)
            gpre[j] = grad_pre
            return mm(w2[j], grad_pre, 1, 0)

        @pl.when(is_last)
        def _():
            gbuf[...] = cot_ref[...]
            produce(1, make_grad_last)
            send(1)

        produce(0, make_first)
        send(0)
        arrive(0)

        def forward(j, carry):
            pre = mm(w2[j], block(0, j), 0, 0)
            cumulative = 0.5 * (1.0 + lax.erf(pre * root_half))
            hidden[j] = (pre * cumulative).astype(bf16)
            slope[j] = cumulative + pre * jnp.exp(-0.5 * pre * pre) * norm_density
            return carry

        lax.fori_loop(0, lb, forward, 0)

        @pl.when(not_last)
        def _():
            produce(2, make_down)
            send(2)
            hand_on().wait_recv()
            produce(1, make_grad_last)
            send(1)

        arrive(1)
        produce(3, make_grad_mixed)
        send(3)

        @pl.when(is_last)
        def _():
            produce(2, make_down)
            send(2)

        def grad_second(j, carry):
            value = mm(block(0, j), gpre[j], 1, 1) * factor
            st2[:, j] = value.astype(bf16).reshape(nd, bs // nd, hb)
            return carry

        def grad_down(j, carry):
            value = mm(hidden[j], block(1, j), 1, 1) * factor
            st3[:, j] = value.astype(bf16).reshape(nd, hb // nd, bs)
            return carry

        lax.fori_loop(0, lb, grad_second, 0)
        spread(1)
        lax.fori_loop(0, lb, grad_down, 0)
        spread(2)

        arrive(3)

        def outgoing(i, carry):
            acts = mm(w1[i], block(3, i), 1, 0).T
            gout[:, cols(i)] = (gbuf[:, cols(i)].astype(f32) + acts).astype(bf16)
            return carry

        lax.fori_loop(0, lb, outgoing, 0)

        @pl.when(not_first)
        def _():
            hand_on().start()

        def grad_first(i, carry):
            value = mm(x_ref[:, cols(i)].T, block(3, i), 1, 1) * factor
            st1[:, i] = value.astype(bf16).reshape(nd, bs // nd, bs)
            return carry

        lax.fori_loop(0, lb, grad_first, 0)
        spread(0)
        arrive(2)

        def grad_last(i, carry):
            value = mm(block(2, i), gbuf[:, cols(i)], 1, 0) * factor
            st4[:, i] = value.astype(bf16).reshape(nd, bs // nd, bs)
            return carry

        lax.fori_loop(0, lb, grad_last, 0)
        spread(3)

        for which in range(4):
            for k in range(1, nt):
                a2a(which, k).wait_send()
        for which in range(4):
            own(which).wait()
            for k in range(1, nd):
                share(which, k).wait()

        @pl.when(not_first)
        def _():
            hand_on().wait_send()

    return kernel


def tokens_split(inputs, cotangent, up_first, up_second, down_first, down_second):
    nt, nd, ns = (lax.axis_size(a) for a in ("tensor", "dp", "pipe"))
    tokens, width = cotangent.shape
    lb, bs, hb = up_second.shape[1:]
    tp = -(-tokens // lanes) * lanes
    factor = 1.0 / math.sqrt(tokens * nd)
    pad = ((0, tp - tokens), (0, 0))
    vmem = pl.BlockSpec(memory_space=pltpu.VMEM)
    anywhere = pl.BlockSpec(memory_space=pl.ANY)
    shapes = (
        (nd, lb, bs // nd, bs),
        (nd, lb, bs // nd, hb),
        (nd, lb, hb // nd, bs),
        (nd, lb, bs // nd, bs),
    )
    stride = bs // (nt * lb)
    exchange = (4, nt, lb, lb * stride, tp)
    dma = pltpu.SemaphoreType.DMA
    flops = 2 * tp * lb * bs * (8 * bs + 10 * hb)
    out = pl.pallas_call(
        make_token_kernel((nt, nd, ns, lb, bs, hb, tp), factor),
        out_shape=(jax.ShapeDtypeStruct((tp, width), bf16),)
        + tuple(jax.ShapeDtypeStruct(s, bf16) for s in shapes),
        in_specs=[vmem] * 6,
        out_specs=(vmem,) + (anywhere,) * 4,
        scratch_shapes=[
            pltpu.VMEM((tp, width), bf16),
            pltpu.VMEM(exchange, bf16),
            pltpu.VMEM(exchange, bf16),
            pltpu.VMEM((lb, hb, tp), bf16),
            pltpu.VMEM((lb, hb, tp), f32),
            pltpu.VMEM((lb, hb, tp), bf16),
        ]
        + [pltpu.VMEM(s, bf16) for s in shapes]
        + [
            dma((4, nt)),
            dma((4, nt)),
            dma((4, nd)),
            dma((4, nd)),
            dma((4,)),
            dma,
            dma,
        ],
        compiler_params=pltpu.CompilerParams(
            collective_id=0, has_side_effects=True, vmem_limit_bytes=60 * 1024 * 1024
        ),
        cost_estimate=pl.CostEstimate(
            flops=flops, bytes_accessed=8 * lb * bs * hb, transcendentals=2 * lb * hb * tp
        ),
    )(
        jnp.pad(inputs[0], pad),
        jnp.pad(cotangent, pad),
        up_first[0],
        up_second[0],
        down_first[0],
        down_second[0],
    )
    sums = tuple(jnp.sum(part.astype(f32), axis=0)[None] for part in out[1:])
    return (out[0][None, :tokens],) + sums


def make_block_kernel(sizes, factor):
    nt, nd, ns, nb, bs, hb, tokens = sizes
    group = nt * nd
    stride = bs // (group * nb)
    rows = nb * stride
    total = nd * tokens
    wide = nb * bs
    pieces = hb // bs

    def kernel(
        x_hbm, cot_hbm, h1, h2, h3, h4,
        gout, r1, r2, r3, r4,
        xbuf, gbuf, obuf, w1, w2, w3, w4,
        sbuf, rbuf, hidden, slope, gpre, st1, st2, st3, st4,
        w_sem, a_send, a_recv, d_send, d_recv, own_sem, p_send, p_recv, go,
    ):
        me_t = lax.axis_index("tensor")
        me_d = lax.axis_index("dp")
        me_s = lax.axis_index("pipe")
        me = me_t * nd + me_d
        is_last = me_s == ns - 1
        not_last = me_s < ns - 1
        not_first = me_s > 0
        is_first = me_s == 0

        def loop(start, stop, step):
            def run(k, carry):
                step(k)
                return carry

            lax.fori_loop(start, stop, run, 0)

        mine = pl.ds(me_d * nb, nb)
        loads = [
            pltpu.make_async_copy(source.at[mine], held, w_sem.at[n])
            for n, (source, held) in enumerate(((h1, w1), (h2, w2), (h3, w3), (h4, w4)))
        ]
        for n in (0, 3, 1, 2):
            loads[n].start()

        def member(k):
            peer = lax.rem(me + k, group)
            return peer, {"tensor": lax.div(peer, nd), "dp": lax.rem(peer, nd)}

        barrier = pltpu.get_barrier_semaphore()

        def greet(k):
            pl.semaphore_signal(barrier, inc=1, device_id=member(k)[1], device_id_type=MESH)

        loop(1, group, greet)
        for k in range(1, ns):
            pl.semaphore_signal(
                barrier, inc=1, device_id={"pipe": lax.rem(me_s + k, ns)}, device_id_type=MESH
            )
        pl.semaphore_wait(barrier, group - 1 + ns - 1)

        def wide_cols(d):
            return pl.ds(pl.multiple_of(d * wide, wide), wide)

        def cols(u):
            return pl.ds(u * bs, bs)

        def source_of(which, d):
            if which == 0:
                return x_hbm.at[:, wide_cols(d)]
            if which == 1:
                return cot_hbm.at[:, wide_cols(d)]
            return (st1, st2, st3, st4, obuf)[which - 2].at[d]

        def target_of(which):
            if which == 6:
                return gout.at[:, wide_cols(me_d)]
            return (xbuf, gbuf, r1, r2, r3, r4)[which].at[me_d]

        def share(which, k):
            peer = lax.rem(me_d + k, nd)
            return pltpu.make_async_remote_copy(
                src_ref=source_of(which, peer),
                dst_ref=target_of(which),
                send_sem=d_send.at[which, k],
                recv_sem=d_recv.at[which, k],
                device_id={"dp": peer},
                device_id_type=MESH,
            )

        def own(which):
            return pltpu.make_async_copy(
                source_of(which, me_d), target_of(which), own_sem.at[which]
            )

        def spread(which):
            for k in range(1, nd):
                share(which, k).start()
            own(which).start()

        def gathered(which):
            own(which).wait()
            for k in range(1, nd):
                share(which, k).wait_recv()

        def a2a(which, k):
            peer, where = member(k)
            return pltpu.make_async_remote_copy(
                src_ref=sbuf.at[which, peer],
                dst_ref=rbuf.at[which, me],
                send_sem=a_send.at[which, k],
                recv_sem=a_recv.at[which, k],
                device_id=where,
                device_id_type=MESH,
            )

        def send(which):
            loop(1, group, lambda k: a2a(which, k).start())
            rbuf[which, me] = sbuf[which, me]

        def arrive(which):
            loop(1, group, lambda k: a2a(which, k).wait_recv())

        def produce(which, make):
            parts = [make(u).reshape(group, nb, stride, total) for u in range(nb)]
            sbuf[which] = jnp.concatenate(parts, axis=2).astype(bf16)

        def block(which, j):
            return rbuf[which, :, j].reshape(bs, total)

        def tokens_of(ref, u):
            return ref[:, :, cols(u)].reshape(total, bs)

        def hand_on():
            return pltpu.make_async_remote_copy(
                src_ref=obuf,
                dst_ref=gbuf,
                send_sem=p_send,
                recv_sem=p_recv,
                device_id={"pipe": lax.rem(me_s + ns - 1, ns)},
                device_id_type=MESH,
            )

        def make_first(u):
            return mm(w1[u], tokens_of(xbuf, u), 0, 1)

        def make_grad_last(u):
            return mm(w4[u], tokens_of(gbuf, u), 1, 1)

        def make_down(u):
            return mm(w3[u], hidden[u], 0, 0)

        def make_grad_mixed(u):
            return mm(w2[u], gpre[u], 1, 0)

        def piece(n):
            return lax.div(n, pieces), pl.ds(pl.multiple_of(lax.rem(n, pieces) * bs, bs), bs)

        def tell(which, step):
            pl.semaphore_signal(
                go.at[which], inc=1, device_id={"pipe": me_s + step}, device_id_type=MESH
            )

        def scaled(value, out_rows):
            return (value * factor).astype(bf16).reshape(nd, out_rows // nd, value.shape[1])

        def finish_first():
            for u in range(nb):
                st1[:, u] = scaled(mm(tokens_of(xbuf, u).T, block(3, u), 1, 1), bs)

        def finish_second():
            for u in range(nb):
                st2[:, u] = scaled(mm(block(0, u), gpre[u], 1, 1), bs)

        def finish_down():
            for u in range(nb):
                st3[:, u] = scaled(mm(hidden[u], block(1, u), 1, 1), hb)

        def finish_last():
            for u in range(nb):
                st4[:, u] = scaled(mm(block(2, u), tokens_of(gbuf, u), 1, 0), bs)

        @pl.when(not_last)
        def _():
            pl.semaphore_wait(go.at[0], 1)

        spread(0)

        @pl.when(is_last)
        def _():
            spread(1)

        loads[0].wait()
        gathered(0)
        produce(0, make_first)
        loads[3].wait()

        @pl.when(not_last)
        def _():
            pl.semaphore_wait(go.at[1], 1)

        send(0)

        @pl.when(is_last)
        def _():
            gathered(1)

        @pl.when(not_first)
        def _():
            tell(0, -1)

        @pl.when(is_last)
        def _():
            produce(1, make_grad_last)

        loads[1].wait()
        loads[2].wait()
        arrive(0)

        @pl.when(is_last)
        def _():
            send(1)

        def forward(n):
            u, part = piece(n)
            slope[u, part] = mm(w2[u, :, part], block(0, u), 0, 0)
            start = lax.rem(n, pieces) * bs

            def activate(m):
                at = pl.ds(pl.multiple_of(start + m * tile, tile), tile)
                pre = slope[u, at]
                cumulative = 0.5 + 0.5 * lax.erf(pre * root_half)
                hidden[u, at] = (pre * cumulative).astype(bf16)
                slope[u, at] = cumulative + pre * jnp.exp(-0.5 * pre * pre) * norm_density

            loop(0, bs // tile, activate)

        loop(0, nb * pieces, forward)

        @pl.when(not_last)
        def _():
            produce(2, make_down)
            pl.semaphore_wait(go.at[2], 1)
            send(2)
            hand_on().wait_recv()
            produce(1, make_grad_last)
            send(1)
            arrive(2)
            finish_last()
            spread(5)

        arrive(1)

        @pl.when(not_first)
        def _():
            tell(1, -1)

        @pl.when(not_last)
        def _():
            tell(3, 1)

        @pl.when(is_first)
        def _():
            finish_down()
            spread(4)

        def backward(n):
            u, part = piece(n)
            gpre[u, part] = (mm(w3[u, part], block(1, u), 1, 0) * slope[u, part]).astype(bf16)

        loop(0, nb * pieces, backward)
        produce(3, make_grad_mixed)
        send(3)
        finish_second()

        @pl.when(is_first)
        def _():
            spread(3)

        @pl.when(not_first)
        def _():
            finish_down()

        @pl.when(is_last)
        def _():
            produce(2, make_down)

        arrive(3)

        @pl.when(not_first)
        def _():
            tell(2, -1)

        for u in range(nb):
            acts = mm(block(3, u), w1[u], 0, 1)
            fresh = tokens_of(gbuf, u).astype(f32) + acts
            obuf[:, :, cols(u)] = fresh.astype(bf16).reshape(nd, tokens, bs)

        @pl.when(not_first)
        def _():
            hand_on().start()
            spread(3)
            spread(4)

        spread(6)
        finish_first()
        spread(2)

        @pl.when(not_first)
        def _():
            pl.semaphore_wait(go.at[3], 1)

        @pl.when(is_last)
        def _():
            send(2)
            arrive(2)
            finish_last()
            spread(5)

        for which in range(4):
            loop(1, group, lambda k: a2a(which, k).wait_send())
        for k in range(1, nd):
            share(0, k).wait_send()

        @pl.when(is_last)
        def _():
            for k in range(1, nd):
                share(1, k).wait_send()

        for which in range(2, 7):
            own(which).wait()
            for k in range(1, nd):
                share(which, k).wait()

        @pl.when(not_first)
        def _():
            hand_on().wait_send()

    return kernel


def blocks_split(inputs, cotangent, up_first, up_second, down_first, down_second):
    nt, nd, ns = (lax.axis_size(a) for a in ("tensor", "dp", "pipe"))
    tokens, width = cotangent.shape
    lb, bs, hb = up_second.shape[1:]
    nb = lb // nd
    total = nd * tokens
    factor = 1.0 / math.sqrt(total)
    anywhere = pl.BlockSpec(memory_space=pl.ANY)
    shapes = (
        (nd, nb, bs // nd, bs),
        (nd, nb, bs // nd, hb),
        (nd, nb, hb // nd, bs),
        (nd, nb, bs // nd, bs),
    )
    group = nt * nd
    exchange = (4, group, nb, bs // group, total)
    dma = pltpu.SemaphoreType.DMA
    flops = 2 * total * nb * bs * (8 * bs + 10 * hb)
    out = pl.pallas_call(
        make_block_kernel((nt, nd, ns, nb, bs, hb, tokens), factor),
        out_shape=(jax.ShapeDtypeStruct((tokens, width), bf16),)
        + tuple(jax.ShapeDtypeStruct(s, bf16) for s in shapes),
        in_specs=[anywhere] * 6,
        out_specs=(anywhere,) * 5,
        scratch_shapes=[pltpu.VMEM((nd, tokens, nb * bs), bf16)] * 3
        + [
            pltpu.VMEM((nb, bs, bs), bf16),
            pltpu.VMEM((nb, bs, hb), bf16),
            pltpu.VMEM((nb, hb, bs), bf16),
            pltpu.VMEM((nb, bs, bs), bf16),
            pltpu.VMEM(exchange, bf16),
            pltpu.VMEM(exchange, bf16),
            pltpu.VMEM((nb, hb, total), bf16),
            pltpu.VMEM((nb, hb, total), f32),
            pltpu.VMEM((nb, hb, total), bf16),
        ]
        + [pltpu.VMEM(s, bf16) for s in shapes]
        + [
            dma((4,)),
            dma((4, group)),
            dma((4, group)),
            dma((7, nd)),
            dma((7, nd)),
            dma((7,)),
            dma,
            dma,
            pltpu.SemaphoreType.REGULAR((4,)),
        ],
        compiler_params=pltpu.CompilerParams(
            collective_id=1, has_side_effects=True, vmem_limit_bytes=60 * 1024 * 1024
        ),
        cost_estimate=pl.CostEstimate(
            flops=flops, bytes_accessed=8 * lb * bs * hb, transcendentals=2 * nb * hb * total
        ),
    )(inputs[0], cotangent, up_first[0], up_second[0], down_first[0], down_second[0])
    grads = tuple(
        part.reshape((lb,) + part.shape[2:]).astype(f32)[None] for part in out[1:]
    )
    return (out[0][None],) + grads


def body(inputs, cotangent, up_first, up_second, down_first, down_second):
    arrays = (inputs, cotangent, up_first, up_second, down_first, down_second)
    nd = lax.axis_size("dp")
    tokens = cotangent.shape[0]
    stride = up_first.shape[-1] // (up_first.shape[1] * lax.axis_size("tensor"))
    nb = up_first.shape[1] // nd
    divides = up_first.shape[1] % nd == 0 and nb * stride % 16 == 0 and nb > 0
    if divides and tokens % 16 == 0 and tokens * nd % lanes == 0:
        return blocks_split(*arrays)
    return tokens_split(*arrays)


def solution(mesh):
    return jax.shard_map(
        body,
        mesh=mesh,
        in_specs=(
            P("pipe", "dp", "tensor"),
            P("dp", "tensor"),
            P("pipe", "tensor", None, None),
            P("pipe", "tensor", None, None),
            P("pipe", "tensor", None, None),
            P("pipe", "tensor", None, None),
        ),
        out_specs=(
            P("pipe", "dp", "tensor"),
            P("pipe", "tensor", "dp", None),
            P("pipe", "tensor", "dp", None),
            P("pipe", "tensor", "dp", None),
            P("pipe", "tensor", "dp", None),
        ),
        check_vma=False,
    )
```

```python
import math

import jax
import jax.numpy as jnp
from jax import lax
from jax.experimental import pallas as pl
from jax.experimental.pallas import tpu as pltpu
from jax.sharding import PartitionSpec as P

MESH = pl.DeviceIdType.MESH
root_half = 1.0 / math.sqrt(2.0)
norm_density = 1.0 / math.sqrt(2.0 * math.pi)
lanes = 128
tile = 16
f32 = jnp.float32
bf16 = jnp.bfloat16


def mm(left, right, left_dim, right_dim):
    return lax.dot_general(
        left, right, (((left_dim,), (right_dim,)), ((), ())), preferred_element_type=f32
    )


def make_token_kernel(sizes, factor):
    nt, nd, ns, lb, bs, hb, tp = sizes
    stride = bs // (nt * lb)
    rows = lb * stride

    def kernel(
        x_ref, cot_ref, w1, w2, w3, w4,
        gout, r1, r2, r3, r4,
        gbuf, sbuf, rbuf, hidden, slope, gpre, st1, st2, st3, st4,
        a_send, a_recv, d_send, d_recv, own_sem, p_send, p_recv,
    ):
        me_t = lax.axis_index("tensor")
        me_d = lax.axis_index("dp")
        me_s = lax.axis_index("pipe")
        is_last = me_s == ns - 1
        not_last = me_s < ns - 1
        not_first = me_s > 0

        barrier = pltpu.get_barrier_semaphore()
        for k in range(1, nt):
            pl.semaphore_signal(
                barrier, inc=1, device_id={"tensor": lax.rem(me_t + k, nt)}, device_id_type=MESH
            )
        for k in range(1, nd):
            pl.semaphore_signal(
                barrier, inc=1, device_id={"dp": lax.rem(me_d + k, nd)}, device_id_type=MESH
            )

        for k in range(1, ns):
            pl.semaphore_signal(
                barrier, inc=1, device_id={"pipe": lax.rem(me_s + k, ns)}, device_id_type=MESH
            )
        pl.semaphore_wait(barrier, nt - 1 + nd - 1 + ns - 1)

        def cols(i):
            return pl.ds(pl.multiple_of(i * bs, bs), bs)

        def produce(which, make):
            def pair(p, carry):
                parts = [make(2 * p + u).reshape(nt, lb, stride, tp) for u in range(2)]
                both = jnp.concatenate(parts, axis=2).astype(bf16)
                at = pl.multiple_of(p * 2 * stride, 2 * stride)
                sbuf[which, :, :, pl.ds(at, 2 * stride), :] = both
                return carry

            lax.fori_loop(0, lb // 2, pair, 0)

        def a2a(which, k):
            peer = lax.rem(me_t + k, nt)
            return pltpu.make_async_remote_copy(
                src_ref=sbuf.at[which, peer],
                dst_ref=rbuf.at[which, me_t],
                send_sem=a_send.at[which, k],
                recv_sem=a_recv.at[which, k],
                device_id={"tensor": peer},
                device_id_type=MESH,
            )

        def send(which):
            for k in range(1, nt):
                a2a(which, k).start()
            rbuf[which, me_t] = sbuf[which, me_t]

        def arrive(which):
            for k in range(1, nt):
                a2a(which, k).wait_recv()

        def block(which, j):
            return rbuf[which, :, j].reshape(bs, tp)

        pairs = ((st1, r1), (st2, r2), (st3, r3), (st4, r4))

        def share(which, k):
            staged, landed = pairs[which]
            peer = lax.rem(me_d + k, nd)
            return pltpu.make_async_remote_copy(
                src_ref=staged.at[peer],
                dst_ref=landed.at[me_d],
                send_sem=d_send.at[which, k],
                recv_sem=d_recv.at[which, k],
                device_id={"dp": peer},
                device_id_type=MESH,
            )

        def own(which):
            staged, landed = pairs[which]
            return pltpu.make_async_copy(staged.at[me_d], landed.at[me_d], own_sem.at[which])

        def spread(which):
            for k in range(1, nd):
                share(which, k).start()
            own(which).start()

        def hand_on():
            return pltpu.make_async_remote_copy(
                src_ref=gout,
                dst_ref=gbuf,
                send_sem=p_send,
                recv_sem=p_recv,
                device_id={"pipe": lax.rem(me_s + ns - 1, ns)},
                device_id_type=MESH,
            )

        def make_first(i):
            return mm(w1[i], x_ref[:, cols(i)], 0, 1)

        def make_grad_last(i):
            return mm(w4[i], gbuf[:, cols(i)], 1, 1)

        def make_down(j):
            return mm(w3[j], hidden[j], 0, 0)

        def make_grad_mixed(j):
            grad_hidden = mm(w3[j], block(1, j), 1, 0)
            grad_pre = (grad_hidden * slope[j]).astype(bf16)
            gpre[j] = grad_pre
            return mm(w2[j], grad_pre, 1, 0)

        @pl.when(is_last)
        def _():
            gbuf[...] = cot_ref[...]
            produce(1, make_grad_last)
            send(1)

        produce(0, make_first)
        send(0)
        arrive(0)

        def forward(j, carry):
            pre = mm(w2[j], block(0, j), 0, 0)
            cumulative = 0.5 * (1.0 + lax.erf(pre * root_half))
            hidden[j] = (pre * cumulative).astype(bf16)
            slope[j] = cumulative + pre * jnp.exp(-0.5 * pre * pre) * norm_density
            return carry

        lax.fori_loop(0, lb, forward, 0)

        @pl.when(not_last)
        def _():
            produce(2, make_down)
            send(2)
            hand_on().wait_recv()
            produce(1, make_grad_last)
            send(1)

        arrive(1)
        produce(3, make_grad_mixed)
        send(3)

        @pl.when(is_last)
        def _():
            produce(2, make_down)
            send(2)

        def grad_second(j, carry):
            value = mm(block(0, j), gpre[j], 1, 1) * factor
            st2[:, j] = value.astype(bf16).reshape(nd, bs // nd, hb)
            return carry

        def grad_down(j, carry):
            value = mm(hidden[j], block(1, j), 1, 1) * factor
            st3[:, j] = value.astype(bf16).reshape(nd, hb // nd, bs)
            return carry

        lax.fori_loop(0, lb, grad_second, 0)
        spread(1)
        lax.fori_loop(0, lb, grad_down, 0)
        spread(2)

        arrive(3)

        def outgoing(i, carry):
            acts = mm(w1[i], block(3, i), 1, 0).T
            gout[:, cols(i)] = (gbuf[:, cols(i)].astype(f32) + acts).astype(bf16)
            return carry

        lax.fori_loop(0, lb, outgoing, 0)

        @pl.when(not_first)
        def _():
            hand_on().start()

        def grad_first(i, carry):
            value = mm(x_ref[:, cols(i)].T, block(3, i), 1, 1) * factor
            st1[:, i] = value.astype(bf16).reshape(nd, bs // nd, bs)
            return carry

        lax.fori_loop(0, lb, grad_first, 0)
        spread(0)
        arrive(2)

        def grad_last(i, carry):
            value = mm(block(2, i), gbuf[:, cols(i)], 1, 0) * factor
            st4[:, i] = value.astype(bf16).reshape(nd, bs // nd, bs)
            return carry

        lax.fori_loop(0, lb, grad_last, 0)
        spread(3)

        for which in range(4):
            for k in range(1, nt):
                a2a(which, k).wait_send()
        for which in range(4):
            own(which).wait()
            for k in range(1, nd):
                share(which, k).wait()

        @pl.when(not_first)
        def _():
            hand_on().wait_send()

    return kernel


def tokens_split(inputs, cotangent, up_first, up_second, down_first, down_second):
    nt, nd, ns = (lax.axis_size(a) for a in ("tensor", "dp", "pipe"))
    tokens, width = cotangent.shape
    lb, bs, hb = up_second.shape[1:]
    tp = -(-tokens // lanes) * lanes
    factor = 1.0 / math.sqrt(tokens * nd)
    pad = ((0, tp - tokens), (0, 0))
    vmem = pl.BlockSpec(memory_space=pltpu.VMEM)
    anywhere = pl.BlockSpec(memory_space=pl.ANY)
    shapes = (
        (nd, lb, bs // nd, bs),
        (nd, lb, bs // nd, hb),
        (nd, lb, hb // nd, bs),
        (nd, lb, bs // nd, bs),
    )
    stride = bs // (nt * lb)
    exchange = (4, nt, lb, lb * stride, tp)
    dma = pltpu.SemaphoreType.DMA
    flops = 2 * tp * lb * bs * (8 * bs + 10 * hb)
    out = pl.pallas_call(
        make_token_kernel((nt, nd, ns, lb, bs, hb, tp), factor),
        out_shape=(jax.ShapeDtypeStruct((tp, width), bf16),)
        + tuple(jax.ShapeDtypeStruct(s, bf16) for s in shapes),
        in_specs=[vmem] * 6,
        out_specs=(vmem,) + (anywhere,) * 4,
        scratch_shapes=[
            pltpu.VMEM((tp, width), bf16),
            pltpu.VMEM(exchange, bf16),
            pltpu.VMEM(exchange, bf16),
            pltpu.VMEM((lb, hb, tp), bf16),
            pltpu.VMEM((lb, hb, tp), f32),
            pltpu.VMEM((lb, hb, tp), bf16),
        ]
        + [pltpu.VMEM(s, bf16) for s in shapes]
        + [
            dma((4, nt)),
            dma((4, nt)),
            dma((4, nd)),
            dma((4, nd)),
            dma((4,)),
            dma,
            dma,
        ],
        compiler_params=pltpu.CompilerParams(
            collective_id=0, has_side_effects=True, vmem_limit_bytes=60 * 1024 * 1024
        ),
        cost_estimate=pl.CostEstimate(
            flops=flops, bytes_accessed=8 * lb * bs * hb, transcendentals=2 * lb * hb * tp
        ),
    )(
        jnp.pad(inputs[0], pad),
        jnp.pad(cotangent, pad),
        up_first[0],
        up_second[0],
        down_first[0],
        down_second[0],
    )
    sums = tuple(jnp.sum(part.astype(f32), axis=0)[None] for part in out[1:])
    return (out[0][None, :tokens],) + sums


def make_block_kernel(sizes, factor):
    nt, nd, ns, nb, bs, hb, tokens = sizes
    group = nt * nd
    stride = bs // (group * nb)
    rows = nb * stride
    total = nd * tokens
    wide = nb * bs
    pieces = hb // bs
    cut = (total // lanes + 1) // 2 * lanes
    spans = (pl.ds(0, cut), pl.ds(cut, total - cut))
    halves = range(2)

    def kernel(
        x_hbm, cot_hbm, h1, h2, h3, h4,
        gout, r1, r2, r3, r4,
        xbuf, gbuf, obuf, w1, w2, w3, w4,
        sbuf, rbuf, hidden, slope, gpre, st1, st2, st3, st4,
        w_sem, a_send, a_recv, d_send, d_recv, own_sem, p_send, p_recv, go,
    ):
        me_t = lax.axis_index("tensor")
        me_d = lax.axis_index("dp")
        me_s = lax.axis_index("pipe")
        me = me_t * nd + me_d
        is_last = me_s == ns - 1
        not_last = me_s < ns - 1
        not_first = me_s > 0
        is_first = me_s == 0

        def loop(start, stop, step):
            def run(k, carry):
                step(k)
                return carry

            lax.fori_loop(start, stop, run, 0)

        mine = pl.ds(me_d * nb, nb)
        loads = [
            pltpu.make_async_copy(source.at[mine], held, w_sem.at[n])
            for n, (source, held) in enumerate(((h1, w1), (h2, w2), (h3, w3), (h4, w4)))
        ]
        for n in (0, 3, 1, 2):
            loads[n].start()

        def member(k):
            peer = lax.rem(me + k, group)
            return peer, {"tensor": lax.div(peer, nd), "dp": lax.rem(peer, nd)}

        barrier = pltpu.get_barrier_semaphore()

        def greet(k):
            pl.semaphore_signal(barrier, inc=1, device_id=member(k)[1], device_id_type=MESH)

        loop(1, group, greet)
        for k in range(1, ns):
            pl.semaphore_signal(
                barrier, inc=1, device_id={"pipe": lax.rem(me_s + k, ns)}, device_id_type=MESH
            )
        pl.semaphore_wait(barrier, group - 1 + ns - 1)

        def wide_cols(d):
            return pl.ds(pl.multiple_of(d * wide, wide), wide)

        def token_rows(d):
            return pl.ds(pl.multiple_of(d * tokens, tile), tokens)

        def cols(u):
            return pl.ds(u * bs, bs)

        def source_of(which, d):
            if which == 0:
                return x_hbm.at[:, wide_cols(d)]
            if which == 1:
                return cot_hbm.at[:, wide_cols(d)]
            if which == 6:
                return obuf.at[token_rows(d)]
            return (st1, st2, st3, st4)[which - 2].at[d]

        def target_of(which):
            if which == 6:
                return gout.at[:, wide_cols(me_d)]
            if which < 2:
                return (xbuf, gbuf)[which].at[token_rows(me_d)]
            return (r1, r2, r3, r4)[which - 2].at[me_d]

        def share(which, k):
            peer = lax.rem(me_d + k, nd)
            return pltpu.make_async_remote_copy(
                src_ref=source_of(which, peer),
                dst_ref=target_of(which),
                send_sem=d_send.at[which, k],
                recv_sem=d_recv.at[which, k],
                device_id={"dp": peer},
                device_id_type=MESH,
            )

        def own(which):
            return pltpu.make_async_copy(
                source_of(which, me_d), target_of(which), own_sem.at[which]
            )

        def spread(which):
            for k in range(1, nd):
                share(which, k).start()
            own(which).start()

        def gathered(which):
            own(which).wait()
            for k in range(1, nd):
                share(which, k).wait_recv()

        def a2a(which, h, k):
            peer, where = member(k)
            return pltpu.make_async_remote_copy(
                src_ref=sbuf.at[which, peer, :, :, spans[h]],
                dst_ref=rbuf.at[which, me, :, :, spans[h]],
                send_sem=a_send.at[which, h, k],
                recv_sem=a_recv.at[which, h, k],
                device_id=where,
                device_id_type=MESH,
            )

        def send(which, h):
            loop(1, group, lambda k: a2a(which, h, k).start())
            rbuf[which, me, :, :, spans[h]] = sbuf[which, me, :, :, spans[h]]

        def arrive(which, h):
            loop(1, group, lambda k: a2a(which, h, k).wait_recv())

        def produce(which, make, h):
            parts = [make(u, h).reshape(group, nb, stride, spans[h].size) for u in range(nb)]
            sbuf[which, :, :, :, spans[h]] = jnp.concatenate(parts, axis=2).astype(bf16)

        def block(which, j):
            return rbuf[which, :, j].reshape(bs, total)

        def part_block(which, j, h):
            return rbuf[which, :, j, :, spans[h]].reshape(bs, spans[h].size)

        def hand_on(h):
            return pltpu.make_async_remote_copy(
                src_ref=obuf.at[spans[h]],
                dst_ref=gbuf.at[spans[h]],
                send_sem=p_send.at[h],
                recv_sem=p_recv.at[h],
                device_id={"pipe": lax.rem(me_s + ns - 1, ns)},
                device_id_type=MESH,
            )

        def make_first(u, h):
            return mm(w1[u], xbuf[spans[h], cols(u)], 0, 1)

        def make_grad_last(u, h):
            return mm(w4[u], gbuf[spans[h], cols(u)], 1, 1)

        def make_down(u, h):
            return mm(w3[u], hidden[u, :, spans[h]], 0, 0)

        def make_grad_mixed(u, h):
            return mm(w2[u], gpre[u, :, spans[h]], 1, 0)

        def piece(n):
            return lax.div(n, pieces), pl.ds(pl.multiple_of(lax.rem(n, pieces) * bs, bs), bs)

        def tell(which, step):
            pl.semaphore_signal(
                go.at[which], inc=1, device_id={"pipe": me_s + step}, device_id_type=MESH
            )

        def scaled(value, out_rows):
            return (value * factor).astype(bf16).reshape(nd, out_rows // nd, value.shape[1])

        def finish_first():
            for u in range(nb):
                st1[:, u] = scaled(mm(xbuf[:, cols(u)].T, block(3, u), 1, 1), bs)

        def finish_second():
            for u in range(nb):
                st2[:, u] = scaled(mm(block(0, u), gpre[u], 1, 1), bs)

        def finish_down():
            for u in range(nb):
                st3[:, u] = scaled(mm(hidden[u], block(1, u), 1, 1), hb)

        def finish_last():
            for u in range(nb):
                st4[:, u] = scaled(mm(block(2, u), gbuf[:, cols(u)], 1, 0), bs)

        @pl.when(not_last)
        def _():
            pl.semaphore_wait(go.at[0], 1)

        spread(0)

        @pl.when(is_last)
        def _():
            spread(1)

        def forward(h):
            def one(n):
                u, part = piece(n)
                slope[u, part, spans[h]] = mm(w2[u, :, part], part_block(0, u, h), 0, 0)
                start = lax.rem(n, pieces) * bs

                def activate(m):
                    at = pl.ds(pl.multiple_of(start + m * tile, tile), tile)
                    pre = slope[u, at, spans[h]]
                    cumulative = 0.5 + 0.5 * lax.erf(pre * root_half)
                    hidden[u, at, spans[h]] = (pre * cumulative).astype(bf16)
                    density = jnp.exp(-0.5 * pre * pre) * norm_density
                    slope[u, at, spans[h]] = cumulative + pre * density

                loop(0, bs // tile, activate)

            loop(0, nb * pieces, one)

        def backward(h):
            def one(n):
                u, part = piece(n)
                grad_hidden = mm(w3[u, part], part_block(1, u, h), 1, 0)
                gpre[u, part, spans[h]] = (grad_hidden * slope[u, part, spans[h]]).astype(bf16)

            loop(0, nb * pieces, one)

        def outgoing(h):
            for u in range(nb):
                acts = mm(part_block(3, u, h), w1[u], 0, 1)
                fresh = gbuf[spans[h], cols(u)].astype(f32) + acts
                obuf[spans[h], cols(u)] = fresh.astype(bf16)

        loads[0].wait()
        gathered(0)

        @pl.when(not_last)
        def _():
            pl.semaphore_wait(go.at[1], 1)

        for h in halves:
            produce(0, make_first, h)
            send(0, h)

        @pl.when(is_last)
        def _():
            gathered(1)

        @pl.when(not_first)
        def _():
            tell(0, -1)

        loads[3].wait()

        @pl.when(is_last)
        def _():
            for h in halves:
                produce(1, make_grad_last, h)

        loads[1].wait()
        loads[2].wait()
        arrive(0, 0)

        @pl.when(is_last)
        def _():
            send(1, 0)

        forward(0)
        arrive(0, 1)

        @pl.when(is_last)
        def _():
            send(1, 1)

        @pl.when(not_last)
        def _():
            forward(1)
            for h in halves:
                produce(2, make_down, h)
                send(2, h)
            for h in halves:
                hand_on(h).wait_recv()
                produce(1, make_grad_last, h)
                send(1, h)

        arrive(1, 0)
        backward(0)
        produce(3, make_grad_mixed, 0)
        send(3, 0)

        @pl.when(is_last)
        def _():
            forward(1)

        arrive(1, 1)

        @pl.when(not_first)
        def _():
            tell(1, -1)

        @pl.when(not_last)
        def _():
            tell(2, 1)

        backward(1)
        produce(3, make_grad_mixed, 1)
        send(3, 1)

        @pl.when(is_first)
        def _():
            finish_down()
            spread(4)
            finish_second()
            spread(3)

        @pl.when(not_last)
        def _():
            for h in halves:
                arrive(2, h)
            finish_last()
            spread(5)

        for h in halves:
            arrive(3, h)
            outgoing(h)

            @pl.when(not_first)
            def _():
                hand_on(h).start()

        spread(6)
        finish_first()
        spread(2)

        @pl.when(not_first)
        def _():
            finish_down()
            spread(4)
            finish_second()
            spread(3)

        @pl.when(is_last)
        def _():
            for h in halves:
                produce(2, make_down, h)

        @pl.when(not_first)
        def _():
            pl.semaphore_wait(go.at[2], 1)

        @pl.when(is_last)
        def _():
            for h in halves:
                send(2, h)
            for h in halves:
                arrive(2, h)
            finish_last()
            spread(5)

        for which in range(4):
            for h in halves:
                loop(1, group, lambda k: a2a(which, h, k).wait_send())
        for k in range(1, nd):
            share(0, k).wait_send()

        @pl.when(is_last)
        def _():
            for k in range(1, nd):
                share(1, k).wait_send()

        for which in range(2, 7):
            own(which).wait()
            for k in range(1, nd):
                share(which, k).wait()

        @pl.when(not_first)
        def _():
            for h in halves:
                hand_on(h).wait_send()

    return kernel


def blocks_split(inputs, cotangent, up_first, up_second, down_first, down_second):
    nt, nd, ns = (lax.axis_size(a) for a in ("tensor", "dp", "pipe"))
    tokens, width = cotangent.shape
    lb, bs, hb = up_second.shape[1:]
    nb = lb // nd
    total = nd * tokens
    factor = 1.0 / math.sqrt(total)
    anywhere = pl.BlockSpec(memory_space=pl.ANY)
    shapes = (
        (nd, nb, bs // nd, bs),
        (nd, nb, bs // nd, hb),
        (nd, nb, hb // nd, bs),
        (nd, nb, bs // nd, bs),
    )
    group = nt * nd
    exchange = (4, group, nb, bs // group, total)
    dma = pltpu.SemaphoreType.DMA
    flops = 2 * total * nb * bs * (8 * bs + 10 * hb)
    out = pl.pallas_call(
        make_block_kernel((nt, nd, ns, nb, bs, hb, tokens), factor),
        out_shape=(jax.ShapeDtypeStruct((tokens, width), bf16),)
        + tuple(jax.ShapeDtypeStruct(s, bf16) for s in shapes),
        in_specs=[anywhere] * 6,
        out_specs=(anywhere,) * 5,
        scratch_shapes=[pltpu.VMEM((total, nb * bs), bf16)] * 3
        + [
            pltpu.VMEM((nb, bs, bs), bf16),
            pltpu.VMEM((nb, bs, hb), bf16),
            pltpu.VMEM((nb, hb, bs), bf16),
            pltpu.VMEM((nb, bs, bs), bf16),
            pltpu.VMEM(exchange, bf16),
            pltpu.VMEM(exchange, bf16),
            pltpu.VMEM((nb, hb, total), bf16),
            pltpu.VMEM((nb, hb, total), f32),
            pltpu.VMEM((nb, hb, total), bf16),
        ]
        + [pltpu.VMEM(s, bf16) for s in shapes]
        + [
            dma((4,)),
            dma((4, 2, group)),
            dma((4, 2, group)),
            dma((7, nd)),
            dma((7, nd)),
            dma((7,)),
            dma((2,)),
            dma((2,)),
            pltpu.SemaphoreType.REGULAR((3,)),
        ],
        compiler_params=pltpu.CompilerParams(
            collective_id=1, has_side_effects=True, vmem_limit_bytes=60 * 1024 * 1024
        ),
        cost_estimate=pl.CostEstimate(
            flops=flops, bytes_accessed=8 * lb * bs * hb, transcendentals=2 * nb * hb * total
        ),
    )(inputs[0], cotangent, up_first[0], up_second[0], down_first[0], down_second[0])
    grads = tuple(
        part.reshape((lb,) + part.shape[2:]).astype(f32)[None] for part in out[1:]
    )
    return (out[0][None],) + grads


def body(inputs, cotangent, up_first, up_second, down_first, down_second):
    arrays = (inputs, cotangent, up_first, up_second, down_first, down_second)
    nd = lax.axis_size("dp")
    tokens = cotangent.shape[0]
    stride = up_first.shape[-1] // (up_first.shape[1] * lax.axis_size("tensor"))
    nb = up_first.shape[1] // nd
    divides = up_first.shape[1] % nd == 0 and nb * stride % 16 == 0 and nb > 0
    if divides and tokens % 16 == 0 and tokens * nd % lanes == 0 and tokens * nd > lanes:
        return blocks_split(*arrays)
    return tokens_split(*arrays)


def solution(mesh):
    return jax.shard_map(
        body,
        mesh=mesh,
        in_specs=(
            P("pipe", "dp", "tensor"),
            P("dp", "tensor"),
            P("pipe", "tensor", None, None),
            P("pipe", "tensor", None, None),
            P("pipe", "tensor", None, None),
            P("pipe", "tensor", None, None),
        ),
        out_specs=(
            P("pipe", "dp", "tensor"),
            P("pipe", "tensor", "dp", None),
            P("pipe", "tensor", "dp", None),
            P("pipe", "tensor", "dp", None),
            P("pipe", "tensor", "dp", None),
        ),
        check_vma=False,
    )
```

```python
import math

import jax
import jax.numpy as jnp
from jax import lax
from jax.experimental import pallas as pl
from jax.experimental.pallas import tpu as pltpu
from jax.sharding import PartitionSpec as P

MESH = pl.DeviceIdType.MESH
root_half = 1.0 / math.sqrt(2.0)
norm_density = 1.0 / math.sqrt(2.0 * math.pi)
lanes = 128
tile = 16
f32 = jnp.float32
bf16 = jnp.bfloat16


def mm(left, right, left_dim, right_dim):
    return lax.dot_general(
        left, right, (((left_dim,), (right_dim,)), ((), ())), preferred_element_type=f32
    )


def make_token_kernel(sizes, factor):
    nt, nd, ns, lb, bs, hb, tp = sizes
    stride = bs // (nt * lb)
    rows = lb * stride

    def kernel(
        x_ref, cot_ref, w1, w2, w3, w4,
        gout, r1, r2, r3, r4,
        gbuf, sbuf, rbuf, hidden, slope, gpre, st1, st2, st3, st4,
        a_send, a_recv, d_send, d_recv, own_sem, p_send, p_recv,
    ):
        me_t = lax.axis_index("tensor")
        me_d = lax.axis_index("dp")
        me_s = lax.axis_index("pipe")
        is_last = me_s == ns - 1
        not_last = me_s < ns - 1
        not_first = me_s > 0

        barrier = pltpu.get_barrier_semaphore()
        for k in range(1, nt):
            pl.semaphore_signal(
                barrier, inc=1, device_id={"tensor": lax.rem(me_t + k, nt)}, device_id_type=MESH
            )
        for k in range(1, nd):
            pl.semaphore_signal(
                barrier, inc=1, device_id={"dp": lax.rem(me_d + k, nd)}, device_id_type=MESH
            )

        for k in range(1, ns):
            pl.semaphore_signal(
                barrier, inc=1, device_id={"pipe": lax.rem(me_s + k, ns)}, device_id_type=MESH
            )
        pl.semaphore_wait(barrier, nt - 1 + nd - 1 + ns - 1)

        def cols(i):
            return pl.ds(pl.multiple_of(i * bs, bs), bs)

        def produce(which, make):
            def pair(p, carry):
                parts = [make(2 * p + u).reshape(nt, lb, stride, tp) for u in range(2)]
                both = jnp.concatenate(parts, axis=2).astype(bf16)
                at = pl.multiple_of(p * 2 * stride, 2 * stride)
                sbuf[which, :, :, pl.ds(at, 2 * stride), :] = both
                return carry

            lax.fori_loop(0, lb // 2, pair, 0)

        def a2a(which, k):
            peer = lax.rem(me_t + k, nt)
            return pltpu.make_async_remote_copy(
                src_ref=sbuf.at[which, peer],
                dst_ref=rbuf.at[which, me_t],
                send_sem=a_send.at[which, k],
                recv_sem=a_recv.at[which, k],
                device_id={"tensor": peer},
                device_id_type=MESH,
            )

        def send(which):
            for k in range(1, nt):
                a2a(which, k).start()
            rbuf[which, me_t] = sbuf[which, me_t]

        def arrive(which):
            for k in range(1, nt):
                a2a(which, k).wait_recv()

        def block(which, j):
            return rbuf[which, :, j].reshape(bs, tp)

        pairs = ((st1, r1), (st2, r2), (st3, r3), (st4, r4))

        def share(which, k):
            staged, landed = pairs[which]
            peer = lax.rem(me_d + k, nd)
            return pltpu.make_async_remote_copy(
                src_ref=staged.at[peer],
                dst_ref=landed.at[me_d],
                send_sem=d_send.at[which, k],
                recv_sem=d_recv.at[which, k],
                device_id={"dp": peer},
                device_id_type=MESH,
            )

        def own(which):
            staged, landed = pairs[which]
            return pltpu.make_async_copy(staged.at[me_d], landed.at[me_d], own_sem.at[which])

        def spread(which):
            for k in range(1, nd):
                share(which, k).start()
            own(which).start()

        def hand_on():
            return pltpu.make_async_remote_copy(
                src_ref=gout,
                dst_ref=gbuf,
                send_sem=p_send,
                recv_sem=p_recv,
                device_id={"pipe": lax.rem(me_s + ns - 1, ns)},
                device_id_type=MESH,
            )

        def make_first(i):
            return mm(w1[i], x_ref[:, cols(i)], 0, 1)

        def make_grad_last(i):
            return mm(w4[i], gbuf[:, cols(i)], 1, 1)

        def make_down(j):
            return mm(w3[j], hidden[j], 0, 0)

        def make_grad_mixed(j):
            grad_hidden = mm(w3[j], block(1, j), 1, 0)
            grad_pre = (grad_hidden * slope[j]).astype(bf16)
            gpre[j] = grad_pre
            return mm(w2[j], grad_pre, 1, 0)

        @pl.when(is_last)
        def _():
            gbuf[...] = cot_ref[...]
            produce(1, make_grad_last)
            send(1)

        produce(0, make_first)
        send(0)
        arrive(0)

        def forward(j, carry):
            pre = mm(w2[j], block(0, j), 0, 0)
            cumulative = 0.5 * (1.0 + lax.erf(pre * root_half))
            hidden[j] = (pre * cumulative).astype(bf16)
            slope[j] = cumulative + pre * jnp.exp(-0.5 * pre * pre) * norm_density
            return carry

        lax.fori_loop(0, lb, forward, 0)

        @pl.when(not_last)
        def _():
            produce(2, make_down)
            send(2)
            hand_on().wait_recv()
            produce(1, make_grad_last)
            send(1)

        arrive(1)
        produce(3, make_grad_mixed)
        send(3)

        @pl.when(is_last)
        def _():
            produce(2, make_down)
            send(2)

        def grad_second(j, carry):
            value = mm(block(0, j), gpre[j], 1, 1) * factor
            st2[:, j] = value.astype(bf16).reshape(nd, bs // nd, hb)
            return carry

        def grad_down(j, carry):
            value = mm(hidden[j], block(1, j), 1, 1) * factor
            st3[:, j] = value.astype(bf16).reshape(nd, hb // nd, bs)
            return carry

        lax.fori_loop(0, lb, grad_second, 0)
        spread(1)
        lax.fori_loop(0, lb, grad_down, 0)
        spread(2)

        arrive(3)

        def outgoing(i, carry):
            acts = mm(w1[i], block(3, i), 1, 0).T
            gout[:, cols(i)] = (gbuf[:, cols(i)].astype(f32) + acts).astype(bf16)
            return carry

        lax.fori_loop(0, lb, outgoing, 0)

        @pl.when(not_first)
        def _():
            hand_on().start()

        def grad_first(i, carry):
            value = mm(x_ref[:, cols(i)].T, block(3, i), 1, 1) * factor
            st1[:, i] = value.astype(bf16).reshape(nd, bs // nd, bs)
            return carry

        lax.fori_loop(0, lb, grad_first, 0)
        spread(0)
        arrive(2)

        def grad_last(i, carry):
            value = mm(block(2, i), gbuf[:, cols(i)], 1, 0) * factor
            st4[:, i] = value.astype(bf16).reshape(nd, bs // nd, bs)
            return carry

        lax.fori_loop(0, lb, grad_last, 0)
        spread(3)

        for which in range(4):
            for k in range(1, nt):
                a2a(which, k).wait_send()
        for which in range(4):
            own(which).wait()
            for k in range(1, nd):
                share(which, k).wait()

        @pl.when(not_first)
        def _():
            hand_on().wait_send()

    return kernel


def tokens_split(inputs, cotangent, up_first, up_second, down_first, down_second):
    nt, nd, ns = (lax.axis_size(a) for a in ("tensor", "dp", "pipe"))
    tokens, width = cotangent.shape
    lb, bs, hb = up_second.shape[1:]
    tp = -(-tokens // lanes) * lanes
    factor = 1.0 / math.sqrt(tokens * nd)
    pad = ((0, tp - tokens), (0, 0))
    vmem = pl.BlockSpec(memory_space=pltpu.VMEM)
    anywhere = pl.BlockSpec(memory_space=pl.ANY)
    shapes = (
        (nd, lb, bs // nd, bs),
        (nd, lb, bs // nd, hb),
        (nd, lb, hb // nd, bs),
        (nd, lb, bs // nd, bs),
    )
    stride = bs // (nt * lb)
    exchange = (4, nt, lb, lb * stride, tp)
    dma = pltpu.SemaphoreType.DMA
    flops = 2 * tp * lb * bs * (8 * bs + 10 * hb)
    out = pl.pallas_call(
        make_token_kernel((nt, nd, ns, lb, bs, hb, tp), factor),
        out_shape=(jax.ShapeDtypeStruct((tp, width), bf16),)
        + tuple(jax.ShapeDtypeStruct(s, bf16) for s in shapes),
        in_specs=[vmem] * 6,
        out_specs=(vmem,) + (anywhere,) * 4,
        scratch_shapes=[
            pltpu.VMEM((tp, width), bf16),
            pltpu.VMEM(exchange, bf16),
            pltpu.VMEM(exchange, bf16),
            pltpu.VMEM((lb, hb, tp), bf16),
            pltpu.VMEM((lb, hb, tp), f32),
            pltpu.VMEM((lb, hb, tp), bf16),
        ]
        + [pltpu.VMEM(s, bf16) for s in shapes]
        + [
            dma((4, nt)),
            dma((4, nt)),
            dma((4, nd)),
            dma((4, nd)),
            dma((4,)),
            dma,
            dma,
        ],
        compiler_params=pltpu.CompilerParams(
            collective_id=0, has_side_effects=True, vmem_limit_bytes=60 * 1024 * 1024
        ),
        cost_estimate=pl.CostEstimate(
            flops=flops, bytes_accessed=8 * lb * bs * hb, transcendentals=2 * lb * hb * tp
        ),
    )(
        jnp.pad(inputs[0], pad),
        jnp.pad(cotangent, pad),
        up_first[0],
        up_second[0],
        down_first[0],
        down_second[0],
    )
    sums = tuple(jnp.sum(part.astype(f32), axis=0)[None] for part in out[1:])
    return (out[0][None, :tokens],) + sums


def make_block_kernel(sizes, factor):
    nt, nd, ns, nb, bs, hb, tokens = sizes
    group = nt * nd
    stride = bs // (group * nb)
    rows = nb * stride
    total = nd * tokens
    wide = nb * bs
    pieces = hb // bs
    cut = (total // lanes + 1) // 2 * lanes
    spans = (pl.ds(0, cut), pl.ds(cut, total - cut))
    halves = range(2)

    def kernel(
        x_hbm, cot_hbm, h1, h2, h3, h4,
        gout, r1, r2, r3, r4,
        xbuf, gbuf, obuf, w1, w2, w3, w4,
        sbuf, rbuf, hidden, slope, gpre, st1, st2, st3, st4,
        w_sem, a_send, a_recv, d_send, d_recv, own_sem, p_send, p_recv, go,
    ):
        me_t = lax.axis_index("tensor")
        me_d = lax.axis_index("dp")
        me_s = lax.axis_index("pipe")
        me = me_t * nd + me_d
        is_last = me_s == ns - 1
        not_last = me_s < ns - 1
        not_first = me_s > 0
        is_first = me_s == 0

        def loop(start, stop, step):
            def run(k, carry):
                step(k)
                return carry

            lax.fori_loop(start, stop, run, 0)

        mine = pl.ds(me_d * nb, nb)
        loads = [
            pltpu.make_async_copy(source.at[mine], held, w_sem.at[n])
            for n, (source, held) in enumerate(((h1, w1), (h2, w2), (h3, w3), (h4, w4)))
        ]
        for n in (0, 3, 1, 2):
            loads[n].start()

        def member(k):
            peer = lax.rem(me + k, group)
            return peer, {"tensor": lax.div(peer, nd), "dp": lax.rem(peer, nd)}

        barrier = pltpu.get_barrier_semaphore()

        def greet(k):
            pl.semaphore_signal(barrier, inc=1, device_id=member(k)[1], device_id_type=MESH)

        loop(1, group, greet)
        for k in range(1, ns):
            pl.semaphore_signal(
                barrier, inc=1, device_id={"pipe": lax.rem(me_s + k, ns)}, device_id_type=MESH
            )
        pl.semaphore_wait(barrier, group - 1 + ns - 1)

        def wide_cols(d):
            return pl.ds(pl.multiple_of(d * wide, wide), wide)

        def token_rows(d):
            return pl.ds(pl.multiple_of(d * tokens, tile), tokens)

        def cols(u):
            return pl.ds(u * bs, bs)

        def source_of(which, d):
            if which == 0:
                return x_hbm.at[:, wide_cols(d)]
            if which == 1:
                return cot_hbm.at[:, wide_cols(d)]
            if which == 6:
                return obuf.at[token_rows(d)]
            return (st1, st2, st3, st4)[which - 2].at[d]

        def target_of(which):
            if which == 6:
                return gout.at[:, wide_cols(me_d)]
            if which < 2:
                return (xbuf, gbuf)[which].at[token_rows(me_d)]
            return (r1, r2, r3, r4)[which - 2].at[me_d]

        def share(which, k):
            peer = lax.rem(me_d + k, nd)
            return pltpu.make_async_remote_copy(
                src_ref=source_of(which, peer),
                dst_ref=target_of(which),
                send_sem=d_send.at[which, k],
                recv_sem=d_recv.at[which, k],
                device_id={"dp": peer},
                device_id_type=MESH,
            )

        def own(which):
            return pltpu.make_async_copy(
                source_of(which, me_d), target_of(which), own_sem.at[which]
            )

        def spread(which):
            for k in range(1, nd):
                share(which, k).start()
            own(which).start()

        def gathered(which):
            own(which).wait()
            for k in range(1, nd):
                share(which, k).wait_recv()

        def a2a(which, h, k):
            peer, where = member(k)
            return pltpu.make_async_remote_copy(
                src_ref=sbuf.at[which, peer, :, :, spans[h]],
                dst_ref=rbuf.at[which, me, :, :, spans[h]],
                send_sem=a_send.at[which, h, k],
                recv_sem=a_recv.at[which, h, k],
                device_id=where,
                device_id_type=MESH,
            )

        def send(which, h):
            loop(1, group, lambda k: a2a(which, h, k).start())
            rbuf[which, me, :, :, spans[h]] = sbuf[which, me, :, :, spans[h]]

        def arrive(which, h):
            loop(1, group, lambda k: a2a(which, h, k).wait_recv())

        def produce(which, make, h):
            parts = [make(u, h).reshape(group, nb, stride, spans[h].size) for u in range(nb)]
            sbuf[which, :, :, :, spans[h]] = jnp.concatenate(parts, axis=2).astype(bf16)

        def block(which, j):
            return rbuf[which, :, j].reshape(bs, total)

        def part_block(which, j, h):
            return rbuf[which, :, j, :, spans[h]].reshape(bs, spans[h].size)

        def hand_on(h):
            return pltpu.make_async_remote_copy(
                src_ref=obuf.at[spans[h]],
                dst_ref=gbuf.at[spans[h]],
                send_sem=p_send.at[h],
                recv_sem=p_recv.at[h],
                device_id={"pipe": lax.rem(me_s + ns - 1, ns)},
                device_id_type=MESH,
            )

        def make_first(u, h):
            return mm(w1[u], xbuf[spans[h], cols(u)], 0, 1)

        def make_grad_last(u, h):
            return mm(w4[u], gbuf[spans[h], cols(u)], 1, 1)

        def make_down(u, h):
            return mm(w3[u], hidden[u, :, spans[h]], 0, 0)

        def make_grad_mixed(u, h):
            return mm(w2[u], gpre[u, :, spans[h]], 1, 0)

        def piece(n):
            return lax.div(n, pieces), pl.ds(pl.multiple_of(lax.rem(n, pieces) * bs, bs), bs)

        def tell(which, step):
            pl.semaphore_signal(
                go.at[which], inc=1, device_id={"pipe": me_s + step}, device_id_type=MESH
            )

        def scaled(value, out_rows):
            return (value * factor).astype(bf16).reshape(nd, out_rows // nd, value.shape[1])

        def finish_first():
            for u in range(nb):
                st1[:, u] = scaled(mm(xbuf[:, cols(u)].T, block(3, u), 1, 1), bs)

        def finish_second():
            for u in range(nb):
                st2[:, u] = scaled(mm(block(0, u), gpre[u], 1, 1), bs)

        def finish_down():
            for u in range(nb):
                st3[:, u] = scaled(mm(hidden[u], block(1, u), 1, 1), hb)

        def finish_last():
            for u in range(nb):
                st4[:, u] = scaled(mm(block(2, u), gbuf[:, cols(u)], 1, 0), bs)

        @pl.when(not_last)
        def _():
            pl.semaphore_wait(go.at[0], 1)

        spread(0)

        @pl.when(is_last)
        def _():
            spread(1)

        def forward(h):
            def one(n):
                u, part = piece(n)
                slope[u, part, spans[h]] = mm(w2[u, :, part], part_block(0, u, h), 0, 0)
                start = lax.rem(n, pieces) * bs

                def activate(m):
                    at = pl.ds(pl.multiple_of(start + m * tile, tile), tile)
                    pre = slope[u, at, spans[h]]
                    cumulative = 0.5 + 0.5 * lax.erf(pre * root_half)
                    hidden[u, at, spans[h]] = (pre * cumulative).astype(bf16)
                    density = jnp.exp(-0.5 * pre * pre) * norm_density
                    slope[u, at, spans[h]] = cumulative + pre * density

                loop(0, bs // tile, activate)

            loop(0, nb * pieces, one)

        def backward(h):
            def one(n):
                u, part = piece(n)
                grad_hidden = mm(w3[u, part], part_block(1, u, h), 1, 0)
                gpre[u, part, spans[h]] = (grad_hidden * slope[u, part, spans[h]]).astype(bf16)

            loop(0, nb * pieces, one)

        def outgoing(h):
            for u in range(nb):
                acts = mm(part_block(3, u, h), w1[u], 0, 1)
                fresh = gbuf[spans[h], cols(u)].astype(f32) + acts
                obuf[spans[h], cols(u)] = fresh.astype(bf16)

        loads[0].wait()
        gathered(0)

        for h in halves:
            produce(0, make_first, h)
            send(0, h)

        @pl.when(is_last)
        def _():
            gathered(1)

        @pl.when(not_first)
        def _():
            tell(0, -1)

        loads[3].wait()

        @pl.when(is_last)
        def _():
            for h in halves:
                produce(1, make_grad_last, h)

        loads[1].wait()
        loads[2].wait()
        arrive(0, 0)

        @pl.when(is_last)
        def _():
            send(1, 0)

        forward(0)
        arrive(0, 1)

        @pl.when(is_last)
        def _():
            send(1, 1)

        @pl.when(not_last)
        def _():
            forward(1)
            for h in halves:
                hand_on(h).wait_recv()
                produce(1, make_grad_last, h)
                send(1, h)
            for h in halves:
                produce(2, make_down, h)
                send(2, h)

        arrive(1, 0)
        backward(0)
        produce(3, make_grad_mixed, 0)
        send(3, 0)

        @pl.when(is_last)
        def _():
            forward(1)

        arrive(1, 1)

        @pl.when(not_last)
        def _():
            tell(1, 1)

        backward(1)
        produce(3, make_grad_mixed, 1)
        send(3, 1)

        @pl.when(is_first)
        def _():
            finish_down()
            spread(4)
            finish_second()
            spread(3)

        @pl.when(not_last)
        def _():
            for h in halves:
                arrive(2, h)
            finish_last()
            spread(5)

        for h in halves:
            arrive(3, h)
            outgoing(h)

            @pl.when(not_first)
            def _():
                hand_on(h).start()

        spread(6)
        finish_first()
        spread(2)

        @pl.when(not_first)
        def _():
            finish_down()
            spread(4)
            finish_second()
            spread(3)

        @pl.when(is_last)
        def _():
            for h in halves:
                produce(2, make_down, h)

        @pl.when(not_first)
        def _():
            pl.semaphore_wait(go.at[1], 1)

        @pl.when(is_last)
        def _():
            for h in halves:
                send(2, h)
            for h in halves:
                arrive(2, h)
            finish_last()
            spread(5)

        for which in range(4):
            for h in halves:
                loop(1, group, lambda k: a2a(which, h, k).wait_send())
        for k in range(1, nd):
            share(0, k).wait_send()

        @pl.when(is_last)
        def _():
            for k in range(1, nd):
                share(1, k).wait_send()

        for which in range(2, 7):
            own(which).wait()
            for k in range(1, nd):
                share(which, k).wait()

        @pl.when(not_first)
        def _():
            for h in halves:
                hand_on(h).wait_send()

    return kernel


def blocks_split(inputs, cotangent, up_first, up_second, down_first, down_second):
    nt, nd, ns = (lax.axis_size(a) for a in ("tensor", "dp", "pipe"))
    tokens, width = cotangent.shape
    lb, bs, hb = up_second.shape[1:]
    nb = lb // nd
    total = nd * tokens
    factor = 1.0 / math.sqrt(total)
    anywhere = pl.BlockSpec(memory_space=pl.ANY)
    shapes = (
        (nd, nb, bs // nd, bs),
        (nd, nb, bs // nd, hb),
        (nd, nb, hb // nd, bs),
        (nd, nb, bs // nd, bs),
    )
    group = nt * nd
    exchange = (4, group, nb, bs // group, total)
    dma = pltpu.SemaphoreType.DMA
    flops = 2 * total * nb * bs * (8 * bs + 10 * hb)
    out = pl.pallas_call(
        make_block_kernel((nt, nd, ns, nb, bs, hb, tokens), factor),
        out_shape=(jax.ShapeDtypeStruct((tokens, width), bf16),)
        + tuple(jax.ShapeDtypeStruct(s, bf16) for s in shapes),
        in_specs=[anywhere] * 6,
        out_specs=(anywhere,) * 5,
        scratch_shapes=[pltpu.VMEM((total, nb * bs), bf16)] * 3
        + [
            pltpu.VMEM((nb, bs, bs), bf16),
            pltpu.VMEM((nb, bs, hb), bf16),
            pltpu.VMEM((nb, hb, bs), bf16),
            pltpu.VMEM((nb, bs, bs), bf16),
            pltpu.VMEM(exchange, bf16),
            pltpu.VMEM(exchange, bf16),
            pltpu.VMEM((nb, hb, total), bf16),
            pltpu.VMEM((nb, hb, total), f32),
            pltpu.VMEM((nb, hb, total), bf16),
        ]
        + [pltpu.VMEM(s, bf16) for s in shapes]
        + [
            dma((4,)),
            dma((4, 2, group)),
            dma((4, 2, group)),
            dma((7, nd)),
            dma((7, nd)),
            dma((7,)),
            dma((2,)),
            dma((2,)),
            pltpu.SemaphoreType.REGULAR((2,)),
        ],
        compiler_params=pltpu.CompilerParams(
            collective_id=1, has_side_effects=True, vmem_limit_bytes=60 * 1024 * 1024
        ),
        cost_estimate=pl.CostEstimate(
            flops=flops, bytes_accessed=8 * lb * bs * hb, transcendentals=2 * nb * hb * total
        ),
    )(inputs[0], cotangent, up_first[0], up_second[0], down_first[0], down_second[0])
    grads = tuple(
        part.reshape((lb,) + part.shape[2:]).astype(f32)[None] for part in out[1:]
    )
    return (out[0][None],) + grads


def body(inputs, cotangent, up_first, up_second, down_first, down_second):
    arrays = (inputs, cotangent, up_first, up_second, down_first, down_second)
    nd = lax.axis_size("dp")
    tokens = cotangent.shape[0]
    stride = up_first.shape[-1] // (up_first.shape[1] * lax.axis_size("tensor"))
    nb = up_first.shape[1] // nd
    divides = up_first.shape[1] % nd == 0 and nb * stride % 16 == 0 and nb > 0
    if divides and tokens % 16 == 0 and tokens * nd % lanes == 0 and tokens * nd > lanes:
        return blocks_split(*arrays)
    return tokens_split(*arrays)


def solution(mesh):
    return jax.shard_map(
        body,
        mesh=mesh,
        in_specs=(
            P("pipe", "dp", "tensor"),
            P("dp", "tensor"),
            P("pipe", "tensor", None, None),
            P("pipe", "tensor", None, None),
            P("pipe", "tensor", None, None),
            P("pipe", "tensor", None, None),
        ),
        out_specs=(
            P("pipe", "dp", "tensor"),
            P("pipe", "tensor", "dp", None),
            P("pipe", "tensor", "dp", None),
            P("pipe", "tensor", "dp", None),
            P("pipe", "tensor", "dp", None),
        ),
        check_vma=False,
    )
```
